32 devices in a mesh: fsdp: 4 (over y, x), seq: 4 (over z), head: 2 (over core).
Axes of the slice: x: 2, y: 2, z: 4, core: 2. Of those that a mesh axis runs over, the one named last changes fastest.
Arguments:
- hidden: bfloat16 [8, 1024, 1024], P('fsdp', 'seq'), may hold values from -6 to 6
- segment_ids: int32 [8, 1024], P('fsdp'), may hold values from 0 to 6, as said below
- norm_gain: float32 [1024], replicated, may hold values from 0.5 to 1.5
- w_zx: bfloat16 [1024, 2, 2048], P('fsdp', None, 'head'), may hold values from -0.1875 to 0.1875
- w_bcdt: bfloat16 [1024, 288], P('fsdp'), may hold values from -0.1875 to 0.1875
- conv_x: float32 [4, 2048], P(None, 'head'), may hold values from -3 to 3
- conv_x_bias: float32 [2048], P('head'), may hold values from -0.5 to 0.5
- conv_bc: float32 [4, 256], replicated, may hold values from -3 to 3
- conv_bc_bias: float32 [256], replicated, may hold values from -0.5 to 0.5
- dt_bias: float32 [32], P('head'), may hold values from -7 to -2
- a_log: float32 [32], P('head'), may hold values from 0 to 2.7
- d_skip: float32 [32], P('head'), may hold values from 0.5 to 1.5
- gate_gain: float32 [2048], P('head'), may hold values from 0.5 to 1.5
- w_out: bfloat16 [2048, 1024], P('head', 'fsdp'), may hold values from -0.125 to 0.125
- cotangent: bfloat16 [8, 1024, 1024], P('fsdp', 'seq'), may hold values from -6 to 6
Outputs:
- block_out: bfloat16 [8, 1024, 1024], P('fsdp', 'seq')
- grad_hidden: float32 [8, 1024, 1024], P('fsdp', 'seq')
- grad_norm_gain: float32 [1024], replicated
- grad_w_zx: float32 [1024, 2, 2048], P('fsdp', None, 'head')
- grad_w_bcdt: float32 [1024, 288], P('fsdp')
- grad_conv_x: float32 [4, 2048], P(None, 'head')
- grad_conv_x_bias: float32 [2048], P('head')
- grad_conv_bc: float32 [4, 256], replicated
- grad_conv_bc_bias: float32 [256], replicated
- grad_dt_bias: float32 [32], P('head')
- grad_a_log: float32 [32], P('head')
- grad_d_skip: float32 [32], P('head')
- grad_gate_gain: float32 [2048], P('head')
- grad_w_out: float32 [2048, 1024], P('head', 'fsdp')
The draws below stay inside these ranges and needn't reach their ends.
Inputs may be any that keep to these rules, and one draw needn't show every extreme that they name: `segment_ids`: within a sequence the ids count its documents from 0 and never fall; whole documents hold 204 to 2048 tokens, the first and last cut by the sequence's ends; among the 2 sequences of each index of fsdp one is a single document.
All inputs are finite; a program needn't handle non-finite values.
Results may differ from the reference program's by a relative error of at most 0.012.
The reference program's roundings to bfloat16 on the way count: a program that leaves them out, or rounds other values in their place, can miss the bound.
Values may be sent and summed in bfloat16 or wider, within the bound.
No kernel may reach another device: no remote copies, remote signals or barrier semaphores. Data moves between devices by JAX's collectives and lax.ppermute only.
A program may use at most 192 MiB of HBM per device.

```python
import math
import jax
import jax.numpy as jnp
from jax import lax

D = 1024
DI = 2048
P_SIZE = 64
N = 128
NH = 32
KC = 4
SPAN = 256
SEQ_DEV = 2
SEQS = 8
L = 1024
NBC = 288
DOC_LO = 204
DOC_HI = 2048


def draw_segment_ids(key, part):
    key = jax.random.fold_in(key, 7)
    len_key, cut_key, pick_key = jax.random.split(key, 3)
    doc_slots = L // DOC_LO + 2
    lengths = jax.random.randint(len_key, (SEQS, doc_slots), DOC_LO, DOC_HI + 1)
    cut_start = jax.random.randint(cut_key, (SEQS, 1), 0, DOC_LO)
    chosen = jax.random.randint(pick_key, (SEQS // SEQ_DEV, 1), 0, SEQ_DEV)
    member = (jnp.arange(SEQS, dtype=jnp.int32) % SEQ_DEV).reshape(SEQS // SEQ_DEV, SEQ_DEV)
    single_doc = (member == chosen).reshape(SEQS, 1)
    first_group = (jnp.arange(SEQS, dtype=jnp.int32) < SEQ_DEV).reshape(SEQS, 1)
    densest = (member == (chosen + 1) % SEQ_DEV).reshape(SEQS, 1) & first_group
    lengths = jnp.where(densest, DOC_LO, lengths)
    cut_start = jnp.where(densest, DOC_LO - 1, cut_start)
    doc_ends = jnp.cumsum(lengths, axis=1) - cut_start
    places = jnp.arange(L, dtype=jnp.int32)
    seg_ids = jnp.sum((doc_ends[:, None, :] <= places[None, :, None]).astype(jnp.int32), axis=2)
    return jnp.where(single_doc, 0, seg_ids).astype(jnp.int32)


def steps_of(own_key, dims, cuts, least, largest):
    loudness, own = 1.0, jax.random.fold_in(own_key, 6)
    for dim, blocks in cuts:
        draws = jnp.exp(jax.random.uniform(jax.random.fold_in(own, dim), (blocks,), jnp.float32, least / len(cuts), largest / len(cuts)))
        loudness = loudness * jnp.repeat(draws, dims[dim] // blocks).reshape([-1 if axis == dim else 1 for axis in range(len(dims))])
    return loudness


def scatter_about(rng, shape, deviation, limit, cuts=(), kind=jnp.bfloat16):
    entries = jax.random.normal(rng, shape, jnp.float32) * deviation
    if len(cuts) > 0:
        entries = steps_of(rng, shape, cuts, -0.22, 0.18) * entries
    return jnp.clip(entries, min=-limit, max=limit).astype(kind)


def setup_inputs(seed: int = 0) -> dict:
    streams_of = jax.random.split(jax.random.key(seed), 16)
    return {
        "hidden": scatter_about(streams_of[0], (SEQS, L, D), 1.0, 6.0, ((0, 4), (1, 4))),
        "segment_ids": draw_segment_ids(jax.random.fold_in(streams_of[15], 71), 0),
        "norm_gain": jnp.clip(1.0 + 0.1 * jax.random.normal(streams_of[2], (D,), jnp.float32), 0.5, 1.5),
        "w_zx": scatter_about(streams_of[3], (D, 2, DI), D ** -0.5, 0.1875, ((0, 4), (2, 2))),
        "w_bcdt": scatter_about(streams_of[4], (D, NBC), D ** -0.5, 0.1875, ((0, 4),)),
        "conv_x": scatter_about(streams_of[5], (KC, DI), KC ** -0.5, 3.0, ((1, 2),), jnp.float32),
        "conv_x_bias": jnp.clip(jax.random.uniform(streams_of[6], (DI,), jnp.float32, -0.5, 0.5) * steps_of(streams_of[6], (DI,), ((0, 2),), -0.4, 0.0), -0.5, 0.5),
        "conv_bc": scatter_about(streams_of[7], (KC, 2 * N), KC ** -0.5, 3.0, (), jnp.float32),
        "conv_bc_bias": jnp.clip(jax.random.uniform(streams_of[8], (2 * N,), jnp.float32, -0.5, 0.5), -0.5, 0.5),
        "dt_bias": jnp.clip(-7.0 + 5.0 * jax.random.uniform(streams_of[9], (NH,), jnp.float32) ** steps_of(streams_of[9], (NH,), ((0, 2),), -0.2, 0.2), -7.0, -2.0),
        "a_log": jnp.clip(2.7 * jax.random.uniform(streams_of[10], (NH,), jnp.float32) ** steps_of(streams_of[10], (NH,), ((0, 2),), -0.2, 0.2), 0.0, 2.7),
        "d_skip": jnp.clip(0.5 + 1.0 * jax.random.uniform(streams_of[11], (NH,), jnp.float32) ** steps_of(streams_of[11], (NH,), ((0, 2),), -0.2, 0.2), 0.5, 1.5),
        "gate_gain": jnp.clip(1.0 + 0.1 * jax.random.normal(streams_of[12], (DI,), jnp.float32), 0.5, 1.5),
        "w_out": scatter_about(streams_of[13], (DI, D), DI ** -0.5, 0.125, ((0, 2), (1, 4))),
        "cotangent": scatter_about(streams_of[14], (SEQS, L, D), 1.0, 6.0, ((0, 4), (1, 4))),
    }


EPS = 1e-05
HIGH = lax.Precision.HIGHEST

@jax.custom_vjp
def low(v):
    return lax.optimization_barrier(v.astype(jnp.bfloat16)).astype(jnp.float32)

@jax.custom_vjp
def low_back(v):
    return v

def low_keep(v):
    return (low(v), None)

def low_pass(kept, grad):
    return (grad,)

def back_keep(v):
    return (v, None)

def back_low(kept, grad):
    return (low(grad),)
low.defvjp(low_keep, low_pass)
low_back.defvjp(back_keep, back_low)

def conv_layer(extended, conv_weight, conv_bias, seg_wide):
    run_rows = extended.shape[-2] - (KC - 1)
    own_seg = seg_wide[..., KC - 1:]
    pre_act = jnp.zeros(extended.shape[:-2] + (run_rows, extended.shape[-1]), jnp.float32) + conv_bias
    for tap_index in range(KC):
        same_seg = (seg_wide[..., tap_index:tap_index + run_rows] == own_seg).astype(jnp.float32)
        pre_act = pre_act + conv_weight[tap_index] * extended[..., tap_index:tap_index + run_rows, :] * same_seg[..., None]
    return pre_act * jax.nn.sigmoid(pre_act)

def ssd_span(ssm_state, x_heads, b_rows, c_rows, dt_rows, seg_rows, seg_prev, decay_rate, skip_gain):
    block_len = x_heads.shape[0]
    log_decay = jnp.cumsum(dt_rows * decay_rate, axis=0)
    positions = jnp.arange(block_len)
    keep_mask = (positions[:, None] >= positions[None, :]) & (seg_rows[:, None] == seg_rows[None, :])
    keep_wide = keep_mask[:, :, None]
    log_gap = jnp.where(keep_wide, log_decay[:, None, :] - log_decay[None, :, :], 0.0)
    decay_mat = jnp.where(keep_wide, jnp.exp(log_gap), 0.0)
    c_dot_b = jnp.dot(c_rows, b_rows.T, precision=HIGH)
    mix_mat = c_dot_b[:, :, None] * decay_mat * dt_rows[None, :, :]
    y_block = jnp.einsum('tsh,shp->thp', mix_mat, x_heads, precision=HIGH)
    entry_gain = jnp.where((seg_rows == seg_prev)[:, None], jnp.exp(log_decay), 0.0)
    y_block = y_block + entry_gain[:, :, None] * jnp.einsum('tn,hpn->thp', c_rows, ssm_state, precision=HIGH)
    y_block = y_block + skip_gain[None, :, None] * x_heads
    tail_gain = jnp.where((seg_rows == seg_rows[-1])[:, None], jnp.exp(log_decay[-1][None, :] - log_decay), 0.0) * dt_rows
    fresh_state = jnp.einsum('shp,sn->hpn', tail_gain[:, :, None] * x_heads, b_rows, precision=HIGH)
    span_gain = jnp.where(seg_rows[-1] == seg_prev, jnp.exp(log_decay[-1]), 0.0)
    return (span_gain[:, None, None] * ssm_state + fresh_state, y_block)

def mixer_sequence(seq_hidden, seg_ids, parameters):
    norm_gain, w_zx, w_bcdt, conv_x, conv_x_bias, conv_bc, conv_bc_bias, dt_bias, a_log, d_skip, gate_gain, w_out = parameters
    inv_rms = lax.rsqrt(lax.optimization_barrier(jnp.mean(seq_hidden * seq_hidden, axis=-1, keepdims=True)) + EPS)
    normed = low(seq_hidden * inv_rms * norm_gain)
    weight_in = jnp.concatenate([w_zx.reshape(D, 2 * DI), w_bcdt], axis=1)
    projected = low_back(low(jnp.dot(normed, weight_in, precision=HIGH)))
    z_gate = projected[:, :DI]
    xbc_pre = projected[:, DI:2 * DI + 2 * N]
    dt_raw = projected[:, 2 * DI + 2 * N:]
    extended = jnp.concatenate([jnp.zeros((KC - 1, DI + 2 * N), jnp.float32), xbc_pre], axis=0)
    seg_wide = jnp.concatenate([jnp.full((KC - 1,), -1, jnp.int32), seg_ids])
    conv_weight = jnp.concatenate([conv_x, conv_bc], axis=1)
    conv_bias = jnp.concatenate([conv_x_bias, conv_bc_bias])
    conv_out = low(conv_layer(extended, conv_weight, conv_bias, seg_wide))
    x_heads = conv_out[:, :DI].reshape(L, NH, P_SIZE)
    b_rows = conv_out[:, DI:DI + N]
    c_rows = conv_out[:, DI + N:]
    dt_rows = jax.nn.softplus(dt_raw + dt_bias)
    decay_rate = -jnp.exp(a_log)
    blocks = L // SPAN
    seg_blocks = seg_ids.reshape(blocks, SPAN)
    seg_prevs = jnp.concatenate([jnp.full((1,), -1, jnp.int32), seg_blocks[:-1, -1]])

    def span_step(ssm_state, pieces):
        return jax.checkpoint(ssd_span)(ssm_state, pieces[0], pieces[1], pieces[2], pieces[3], pieces[4], pieces[5], decay_rate, d_skip)
    start_state = jnp.zeros((NH, P_SIZE, N), jnp.float32)
    _, y_blocks = lax.scan(span_step, start_state, (x_heads.reshape(blocks, SPAN, NH, P_SIZE), b_rows.reshape(blocks, SPAN, N), c_rows.reshape(blocks, SPAN, N), dt_rows.reshape(blocks, SPAN, NH), seg_blocks, seg_prevs))
    y_flat = y_blocks.reshape(L, DI)
    gated = y_flat * z_gate * jax.nn.sigmoid(z_gate)
    gate_rms = lax.rsqrt(lax.optimization_barrier(jnp.mean(gated * gated, axis=-1, keepdims=True)) + EPS)
    out_norm = low(gated * gate_rms * gate_gain)
    return seq_hidden + jnp.dot(out_norm, w_out, precision=HIGH)

def reference(hidden, segment_ids, norm_gain, w_zx, w_bcdt, conv_x, conv_x_bias, conv_bc, conv_bc_bias, dt_bias, a_log, d_skip, gate_gain, w_out, cotangent):
    parameters = tuple((tensor.astype(jnp.float32) for tensor in (norm_gain, w_zx, w_bcdt, conv_x, conv_x_bias, conv_bc, conv_bc_bias, dt_bias, a_log, d_skip, gate_gain, w_out)))
    group_size = math.gcd(SEQS, max(1, 4096 // L))
    group_count = SEQS // group_size

    def run_group(group_hidden, group_ids, params_in):
        return jax.vmap(mixer_sequence, in_axes=(0, 0, None))(group_hidden, group_ids, params_in)

    def forward(hidden_in, params_in):

        def one_group(pieces):
            return jax.checkpoint(run_group)(pieces[0], pieces[1], params_in)
        result = lax.map(one_group, (hidden_in.reshape(group_count, group_size, L, D), segment_ids.reshape(group_count, group_size, L)))
        return result.reshape(SEQS, L, D)
    block_out, pull_back = jax.vjp(forward, hidden.astype(jnp.float32), parameters)
    grad_hidden, grad_params = pull_back(cotangent.astype(jnp.float32))
    return (block_out.astype(jnp.bfloat16), grad_hidden, grad_params[0], grad_params[1], grad_params[2], grad_params[3], grad_params[4], grad_params[5], grad_params[6], grad_params[7], grad_params[8], grad_params[9], grad_params[10], grad_params[11])
```

```python
import jax
import jax.numpy as jnp
from jax import lax
from jax.sharding import PartitionSpec as P

P_SIZE = 64
N = 128
NH = 32
KC = 4
NBC = 288

EPS = 1e-05
F32 = jnp.float32
BF16 = jnp.bfloat16
EXACT = lax.Precision.HIGHEST


def hop(value, axis, bit):
    return lax.ppermute(value, axis, [(i, i ^ bit) for i in range(lax.axis_size(axis))])


def step_along(value, axis, steps):
    count = lax.axis_size(axis)
    initial, last = (max(0, -steps), min(count, count - steps))
    return lax.ppermute(value, axis, [(source, source + steps) for source in range(initial, last)])


def square(axis):
    return lax.axis_size(axis) == 4


def swap_blocks(value, axis, dim):
    if not square(axis):
        return value
    place = lax.axis_index(axis)
    width = value.shape[dim] // 4
    blocks = [
        lax.dynamic_slice_in_dim(value, jnp.bitwise_xor(place, j) * width, width, dim)
        for j in range(4)
    ]
    return jnp.concatenate(blocks, axis=dim)


def gather_blocks(weight, axis):
    if not square(axis):
        gathered = lax.all_gather(weight, axis)
        return [gathered[i] for i in range(lax.axis_size(axis))]
    half = weight.shape[0] // 2
    one = hop(weight, axis, 1)
    two = hop(weight, axis, 2)
    low = hop(one[:half], axis, 2)
    high = hop(two[half:], axis, 1)
    return [weight, one, two, jnp.concatenate([low, high], axis=0)]


def scatter_blocks(blocks, axis):
    if not square(axis):
        return lax.psum_scatter(jnp.stack(blocks), axis, scatter_dimension=0, tiled=False)
    half = blocks[0].shape[0] // 2
    sent = [b.astype(BF16) for b in blocks[1:]]
    low_one = hop(jnp.concatenate([sent[0][:half], sent[2][:half]], axis=0), axis, 1)
    high_two = hop(jnp.concatenate([sent[1][half:], sent[2][half:]], axis=0), axis, 2)
    low_next = (blocks[2][:half] + low_one[half:]).astype(BF16)
    high_next = (blocks[1][half:] + high_two[half:]).astype(BF16)
    low_two = hop(low_next, axis, 2)
    high_one = hop(high_next, axis, 1)
    return jnp.concatenate(
        [
            blocks[0][:half] + low_one[:half].astype(F32) + low_two.astype(F32),
            blocks[0][half:] + high_two[:half].astype(F32) + high_one.astype(F32),
        ],
        axis=0,
    )


def sum_line(value, axis):
    if not square(axis):
        return lax.psum(value, axis)
    quarter = value.shape[0] // 4
    swapped = swap_blocks(value, axis, 0)
    own = swapped[:quarter]
    for bit in range(1, 4):
        own = own + hop(
            swapped[bit * quarter : (bit + 1) * quarter].astype(BF16), axis, bit
        ).astype(F32)
    own = own.astype(BF16)
    parts = [own] + [hop(own, axis, bit) for bit in range(1, 4)]
    return swap_blocks(jnp.concatenate(parts, axis=0), axis, 0).astype(F32)


def sum_all(value, axes):
    for axis in axes:
        count = lax.axis_size(axis)
        if count & (count - 1):
            value = lax.psum(value, axis)
            continue
        bit = 1
        while bit < count:
            value = value + hop(value, axis, bit)
            bit *= 2
    return value


def shards(
    hidden,
    segment_ids,
    norm_gain,
    w_zx,
    w_bcdt,
    conv_x,
    conv_x_bias,
    conv_bc,
    conv_bc_bias,
    dt_bias,
    a_log,
    d_skip,
    gate_gain,
    w_out,
    cotangent,
):
    head_place = lax.axis_index("head")
    seq_place = lax.axis_index("seq")
    seqs, rows, width = hidden.shape
    inner = w_zx.shape[2]
    heads = dt_bias.shape[0]
    inner_full = inner * lax.axis_size("head")
    tokens = seqs * rows
    lanes = inner + 2 * N

    seg_padded = jnp.concatenate([jnp.full((seqs, KC - 1), -1, jnp.int32), segment_ids], axis=1)
    seg_padded = jnp.concatenate([seg_padded, jnp.full((seqs, KC - 1), -2, jnp.int32)], axis=1)
    seg_wide = lax.dynamic_slice_in_dim(
        seg_padded, seq_place * rows, rows + 2 * (KC - 1), 1
    )
    seg_run = seg_wide[:, KC - 1 : KC - 1 + rows]
    seg_before = seg_wide[:, KC - 2 : KC - 1]
    head_of = jnp.arange(inner) // P_SIZE
    spread = (jnp.arange(heads)[:, None] == head_of[None, :]).astype(F32)

    def widen(v):
        return jnp.dot(v, spread, precision=EXACT)

    def per_head(v):
        return jnp.einsum("...i,hi->...h", v, spread, precision=lax.Precision.HIGH)

    hid = swap_blocks(hidden, "fsdp", 2).reshape(tokens, width).astype(F32)
    gain = swap_blocks(norm_gain, "fsdp", 0)
    cot = swap_blocks(cotangent, "fsdp", 2).reshape(tokens, width)
    inv_rms = lax.rsqrt(jnp.mean(hid * hid, axis=-1, keepdims=True) + EPS)
    normed = (hid * inv_rms * gain).astype(BF16)

    x_blocks = gather_blocks(jnp.concatenate([w_zx[:, 1], w_bcdt], axis=1), "fsdp")
    w_x = jnp.concatenate(x_blocks, axis=0)
    z_own, out_own, _ = lax.optimization_barrier((w_zx[:, 0], w_out, w_x))
    w_z = jnp.concatenate(gather_blocks(z_own, "fsdp"), axis=0)
    w_o = jnp.concatenate(gather_blocks(out_own, "fsdp"), axis=1)

    proj = jnp.dot(normed, w_x, preferred_element_type=F32).astype(BF16)
    proj = proj.reshape(seqs, rows, lanes + NH)
    xbc = proj[..., :lanes]
    dt_raw = lax.dynamic_slice_in_dim(
        proj[..., lanes:], head_place * heads, heads, 2
    ).astype(F32)
    rim = step_along(xbc[:, rows - (KC - 1) :], "seq", 1)
    ext = jnp.concatenate([rim, xbc], axis=1).astype(F32)
    taps = jnp.concatenate([conv_x, conv_bc], axis=1)
    tap_bias = jnp.concatenate([conv_x_bias, conv_bc_bias])
    same = [
        (seg_wide[:, k : k + rows] == seg_run).astype(F32)[..., None] for k in range(KC)
    ]
    pre = tap_bias
    for k in range(KC):
        pre = pre + taps[k] * ext[:, k : k + rows] * same[k]
    pre_sig = jax.nn.sigmoid(pre)
    act = (pre * pre_sig).astype(BF16)
    xs = act[..., :inner]
    bs = act[..., inner : inner + N]
    cs = act[..., inner + N :]

    dt_in = dt_raw + dt_bias
    dt = jax.nn.softplus(dt_in)
    decay = -jnp.exp(a_log)
    lower = jnp.tril(jnp.ones((rows, rows), F32))
    cum = jnp.einsum("ts,bsh->bth", lower, dt * decay, precision=EXACT)
    cum_wide, dt_wide = widen(cum), widen(dt)
    last = cum_wide[:, -1:]
    enter = (seg_run == seg_before)[..., None]
    leave = (seg_run == seg_run[:, -1:])[..., None]
    entry_gain = jnp.where(enter, jnp.exp(cum_wide), 0.0)
    tail_gain = jnp.where(leave, jnp.exp(last - cum_wide), 0.0) * dt_wide
    run_gain = jnp.where(enter[:, -1:], jnp.exp(last), 0.0).reshape(seqs, inner, 1)

    x_tail = (tail_gain * xs).astype(BF16)
    fresh = jnp.einsum("bsi,bsn->bin", x_tail, bs, preferred_element_type=F32)

    def along(own, steps):
        entering = jnp.zeros((seqs, inner, N), BF16)
        leaving = own
        for _ in range(lax.axis_size("seq") - 1):
            entering = step_along(leaving.astype(BF16), "seq", steps)
            leaving = run_gain * entering + own
        return entering, leaving

    state_in, state_out = along(fresh, 1)

    keep = jnp.tril(jnp.ones((rows, rows), bool)) & (seg_run[:, :, None] == seg_run[:, None, :])
    gap = jnp.where(keep[:, None], jnp.swapaxes(cum, 1, 2)[..., None] - jnp.swapaxes(cum, 1, 2)[:, :, None, :], 0.0)
    ldt = jnp.where(keep[:, None], jnp.exp(gap), 0.0) * jnp.swapaxes(dt, 1, 2)[:, :, None, :]
    cb = jnp.einsum("btn,bsn->bts", cs, bs, preferred_element_type=F32)
    mix = (ldt * cb[:, None]).astype(BF16)
    x_heads = xs.reshape(seqs, rows, heads, P_SIZE)
    y_block = jnp.einsum("bhts,bshp->bthp", mix, x_heads, preferred_element_type=F32).reshape(
        seqs, rows, inner
    )
    skip_wide = jnp.repeat(d_skip, P_SIZE)
    y_inter = entry_gain * jnp.einsum("btn,bin->bti", cs, state_in, preferred_element_type=F32)
    y_ssd = y_block + y_inter
    y = y_ssd + skip_wide * xs

    z = (
        jnp.dot(normed, w_z, preferred_element_type=F32)
        .astype(BF16)
        .reshape(seqs, rows, inner)
        .astype(F32)
    )
    z_sig = jax.nn.sigmoid(z)
    z_silu = z * z_sig
    gated = y * z_silu
    d_outn = jnp.einsum("td,id->ti", cot, w_o, preferred_element_type=F32).reshape(
        seqs, rows, inner
    )
    scaled = d_outn * gate_gain
    sums = jnp.stack(
        [jnp.sum(gated * gated, axis=-1), jnp.sum(scaled * gated, axis=-1)], axis=0
    )
    sums = sum_all(sums, ("head",))
    gate_rms = lax.rsqrt(sums[0] / inner_full + EPS)[..., None]
    normal = gated * gate_rms
    out_norm = (normal * gate_gain).astype(BF16).reshape(tokens, inner)
    grad_gate = jnp.sum(d_outn * normal, axis=(0, 1))
    d_gated = scaled * gate_rms - normal * (gate_rms**2 * sums[1][..., None] / inner_full)
    d_y = (d_gated * z_silu).astype(BF16)
    d_z = (d_gated * y * z_sig * (1.0 + z * (1.0 - z_sig))).astype(BF16).reshape(tokens, inner)

    dy_entry = (entry_gain * d_y).astype(BF16)
    back = jnp.einsum("bti,btn->bin", dy_entry, cs, preferred_element_type=F32)
    grad_state, _ = along(back, -1)

    mixed = sum_all(jnp.dot(out_norm, w_o, preferred_element_type=F32), ("head",))
    block_out = swap_blocks((hid + mixed).astype(BF16), "fsdp", 1).reshape(seqs, rows, width)
    grad_o = jnp.einsum("ti,td->id", out_norm, cot, preferred_element_type=F32)
    quarter = width // lax.axis_size("fsdp")
    count = lax.axis_size("fsdp")
    grad_o = scatter_blocks([grad_o[:, j * quarter : (j + 1) * quarter] for j in range(count)], "fsdp")
    grad_z = jnp.einsum("td,tc->dc", normed, d_z, preferred_element_type=F32)
    grad_z = scatter_blocks([grad_z[j * quarter : (j + 1) * quarter] for j in range(count)], "fsdp")
    grad_o = sum_line(grad_o, "seq")
    grad_z = sum_line(grad_z, "seq")

    dy_heads = d_y.reshape(seqs, rows, heads, P_SIZE)
    pair = jnp.einsum("bthp,bshp->bhts", dy_heads, x_heads, preferred_element_type=F32)
    d_cb = jnp.sum(pair * ldt, axis=1).astype(BF16)
    d_c = jnp.einsum("bts,bsn->btn", d_cb, bs, preferred_element_type=F32)
    d_b = jnp.einsum("bts,btn->bsn", d_cb, cs, preferred_element_type=F32)
    back_x = jnp.einsum("bhts,bthp->bshp", mix, dy_heads, preferred_element_type=F32).reshape(
        seqs, rows, inner
    )
    from_state = tail_gain * jnp.einsum(
        "bsn,bin->bsi", bs, grad_state, preferred_element_type=F32
    )
    d_xs = skip_wide * d_y + back_x + from_state
    d_c = d_c + jnp.einsum("bti,bin->btn", dy_entry, state_in, preferred_element_type=F32)
    d_b = d_b + jnp.einsum("bsi,bin->bsn", x_tail, grad_state, preferred_element_type=F32)

    inside = per_head(d_y * y_ssd - xs * back_x)
    outside = per_head(xs * from_state)
    through = jnp.sum(
        (run_gain * grad_state.astype(F32) * state_in).reshape(seqs, heads, P_SIZE * N), axis=-1
    )
    d_decay = (
        jnp.einsum("ts,bth->bsh", lower, inside, precision=EXACT)
        + jnp.einsum("ts,bsh->bth", lower - jnp.eye(rows), outside, precision=EXACT)
        + through[:, None]
    )
    along_x = per_head(xs * (back_x + from_state))
    dt_sig = jax.nn.sigmoid(dt_in)
    ratio = jnp.where(dt_in < -20.0, 1.0, dt_sig / jnp.maximum(dt, 1e-30))
    d_raw = along_x * ratio + decay * d_decay * dt_sig
    grad_dtb = jnp.sum(d_raw, axis=(0, 1))
    grad_alog = decay * jnp.sum(dt * d_decay, axis=(0, 1))
    grad_skip = jnp.sum(per_head(d_y * xs.astype(F32)), axis=(0, 1))

    d_raw_wide = lax.dynamic_update_slice_in_dim(
        jnp.zeros((seqs, rows, NH), F32), d_raw, head_place * heads, 2
    )
    shared = sum_all(jnp.concatenate([d_b, d_c, d_raw_wide], axis=-1), ("head",))

    d_act = jnp.concatenate([d_xs, shared[..., : 2 * N]], axis=-1)
    d_pre = d_act * pre_sig * (1.0 + pre * (1.0 - pre_sig))
    rim_back = step_along(d_pre[:, : KC - 1], "seq", -1)
    d_ext = jnp.concatenate([d_pre, rim_back], axis=1)
    d_xbc = jnp.zeros_like(d_pre)
    for k in range(KC):
        shift = KC - 1 - k
        later = seg_wide[:, KC - 1 + shift : KC - 1 + shift + rows]
        d_xbc = d_xbc + taps[k] * d_ext[:, shift : shift + rows] * (
            later == seg_run
        ).astype(F32)[..., None]
    grad_taps = jnp.stack(
        [jnp.sum(d_pre * ext[:, k : k + rows] * same[k], axis=(0, 1)) for k in range(KC)]
    )
    grad_tap_bias = jnp.sum(d_pre, axis=(0, 1))
    d_xb = jnp.concatenate([d_xbc, shared[..., 2 * N :]], axis=-1).astype(BF16)
    d_xb = d_xb.reshape(tokens, lanes + NH)

    grad_x = jnp.einsum("td,tc->dc", normed, d_xb, preferred_element_type=F32)
    grad_x = scatter_blocks([grad_x[j * quarter : (j + 1) * quarter] for j in range(count)], "fsdp")
    grad_x = sum_line(grad_x, "seq")
    by_head = jnp.einsum("tc,dc->td", d_z, w_z, preferred_element_type=F32) + jnp.einsum(
        "tc,dc->td", d_xb[:, :inner], w_x[:, :inner], preferred_element_type=F32
    )
    d_normed = sum_all(by_head, ("head",)) + jnp.einsum(
        "tc,dc->td", d_xb[:, inner:], w_x[:, inner:], preferred_element_type=F32
    )
    grad_norm = swap_blocks(jnp.sum(d_normed * hid * inv_rms, axis=0), "fsdp", 0)
    q = d_normed * gain
    grad_hidden = (
        cot.astype(F32)
        + q * inv_rms
        - hid * (inv_rms**3 * jnp.sum(q * hid, axis=-1, keepdims=True) / width)
    )
    grad_hidden = swap_blocks(grad_hidden, "fsdp", 1).reshape(seqs, rows, width)

    smalls = [grad_norm, grad_taps, grad_tap_bias, grad_dtb, grad_alog, grad_skip, grad_gate]
    flat = sum_all(jnp.concatenate([s.reshape(-1) for s in smalls]), ("fsdp", "seq"))
    summed = []
    start = 0
    for s in smalls:
        summed.append(flat[start : start + s.size].reshape(s.shape))
        start += s.size
    grad_norm, grad_taps, grad_tap_bias, grad_dtb, grad_alog, grad_skip, grad_gate = summed
    return (
        block_out,
        grad_hidden,
        grad_norm,
        jnp.stack([grad_z, grad_x[:, :inner]], axis=1),
        grad_x[:, inner:],
        grad_taps[:, :inner],
        grad_tap_bias[:inner],
        grad_taps[:, inner:],
        grad_tap_bias[inner:],
        grad_dtb,
        grad_alog,
        grad_skip,
        grad_gate,
        grad_o,
    )


def solution(mesh):
    placed = (
        P("fsdp", "seq", None),
        P("fsdp", None),
        P(),
        P("fsdp", None, "head"),
        P("fsdp", None),
        P(None, "head"),
        P("head"),
        P(),
        P(),
        P("head"),
        P("head"),
        P("head"),
        P("head"),
        P("head", "fsdp"),
        P("fsdp", "seq", None),
    )
    return jax.shard_map(
        shards,
        mesh=mesh,
        in_specs=placed,
        out_specs=(
            P("fsdp", "seq", None),
            P("fsdp", "seq", None),
            P(),
            P("fsdp", None, "head"),
            P("fsdp", None),
            P(None, "head"),
            P("head"),
            P(),
            P(),
            P("head"),
            P("head"),
            P("head"),
            P("head"),
            P("head", "fsdp"),
        ),
        check_vma=False,
    )
```

```python
import functools

import jax
import jax.numpy as jnp
from jax import lax
from jax.experimental import pallas as pl
from jax.experimental.pallas import tpu as pltpu
from jax.sharding import PartitionSpec as P

P_SIZE = 64
N = 128
NH = 32
KC = 4
NBC = 288
TAIL = 384
RIM = 16
PAIR = 128

EPS = 1e-05
F32 = jnp.float32
BF16 = jnp.bfloat16
EXACT = lax.Precision.HIGHEST
VMEM = 24 * 2**20


def hop(value, axis, bit):
    return lax.ppermute(value, axis, [(i, i ^ bit) for i in range(lax.axis_size(axis))])


def step_along(value, axis, steps):
    count = lax.axis_size(axis)
    initial, last = (max(0, -steps), min(count, count - steps))
    return lax.ppermute(value, axis, [(source, source + steps) for source in range(initial, last)])


class Order:
    def __init__(self):
        self.last = None

    def after(self, *values):
        if self.last is None:
            return values
        return lax.optimization_barrier(values + (self.last,))[:-1]

    def did(self, value):
        self.last = value
        return value


def square(axis):
    return lax.axis_size(axis) == 4


def tie(value, *others):
    return lax.optimization_barrier((value,) + others)[0]


def gather_halves(low, high, axis):
    low_one = hop(low, axis, 1)
    high_two = hop(high, axis, 2)
    high_one = hop(high, axis, 1)
    low_two = hop(low, axis, 2)
    low_three = hop(low_one, axis, 2)
    high_three = hop(high_two, axis, 1)
    return [low, high, low_one, high_one, low_two, high_two, low_three, high_three]


def sum_all(value, axes):
    for axis in axes:
        count = lax.axis_size(axis)
        if count & (count - 1):
            value = lax.psum(value, axis)
            continue
        bit = 1
        while bit < count:
            value = value + hop(value, axis, bit)
            bit *= 2
    return value


NT = (((1,), (1,)), ((), ()))
TN = (((0,), (0,)), ((), ()))
NN = (((1,), (0,)), ((), ()))


def mul(a, b, dims=NN, precision=None):
    return lax.dot_general(a, b, dims, precision=precision, preferred_element_type=F32)


def tri(rows, strict=False, upper=False):
    t = lax.broadcasted_iota(jnp.int32, (rows, rows), 0)
    s = lax.broadcasted_iota(jnp.int32, (rows, rows), 1)
    if upper:
        t, s = s, t
    return jnp.where(t > s if strict else t >= s, 1.0, 0.0).astype(F32)


def two(left, right):
    lane = lax.broadcasted_iota(jnp.int32, (1, PAIR), 1)
    return jnp.where(lane < P_SIZE, left, right)


def pair_of(columns, head):
    return two(columns[:, head : head + 1], columns[:, head + 1 : head + 2])


def conv_pre(ext, taps, bias, marks):
    pre = bias + taps[KC - 1 : KC] * ext[RIM:]
    for k in range(KC - 1):
        pre = pre + taps[k : k + 1] * pltpu.roll(ext, KC - 1 - k, 0)[RIM:] * marks[:, k : k + 1]
    return pre


def gains(cum, dt, marks, head):
    rows = cum.shape[0]
    cum_pair = pair_of(cum, head)
    last = two(cum[rows - 1 : rows, head : head + 1], cum[rows - 1 : rows, head + 1 : head + 2])
    entry = marks[:, 6:7] * jnp.exp(cum_pair)
    tail = marks[:, 7:8] * jnp.exp(last - cum_pair) * pair_of(dt, head)
    return entry, tail


def decay_steps(cum, cum_rows, dt_rows, bias, head):
    return (
        jnp.exp(cum[:, head : head + 1] - cum_rows[head : head + 1] + bias)
        * dt_rows[head : head + 1]
    )


def block_lanes(ref, place, j):
    width = ref.shape[1] // 4
    return ref[:, pl.ds(pl.multiple_of(jnp.bitwise_xor(place, j) * width, width), width)]


def both_halves(refs, j, lanes=slice(None)):
    return jnp.concatenate([refs[2 * j][:, lanes], refs[2 * j + 1][:, lanes]], axis=0)


def pack_x_kernel(w_ref, bc_ref, low_ref, high_ref):
    half = w_ref.shape[0] // 2
    inner = w_ref.shape[2]
    low_ref[:, :inner] = w_ref[:half, 1, :]
    high_ref[:, :inner] = w_ref[half:, 1, :]
    turned = bc_ref[...].astype(F32).T.astype(BF16)
    for ref, part in ((low_ref, turned[:half]), (high_ref, turned[half:])):
        ref[:, inner + 2 * N :] = jnp.zeros((half, TAIL - 2 * N), BF16)
        ref[:, inner : inner + NBC] = part


def pack_zo_kernel(w_ref, o_ref, low_ref, high_ref):
    half = w_ref.shape[0] // 2
    inner = w_ref.shape[2]
    low_ref[:, :inner] = w_ref[:half, 0, :]
    high_ref[:, :inner] = w_ref[half:, 0, :]
    turned = o_ref[...].astype(F32).T.astype(BF16)
    low_ref[:, inner:] = turned[:half]
    high_ref[:, inner:] = turned[half:]


def input_kernel(place_ref, rim_ref, n_ref, *refs):
    x_ref, bc_ref, dt_ref = refs[-3:]
    weights = refs[:-3]
    inner = x_ref.shape[1]
    place = place_ref[0]
    proj = 0.0
    for j in range(4):
        rows = jnp.concatenate([block_lanes(rim_ref, place, j), block_lanes(n_ref, place, j)], axis=0)
        proj = proj + mul(rows, both_halves(weights, j))
    x_ref[...] = proj[:, :inner].astype(BF16)
    bc_ref[...] = proj[:, inner : inner + 2 * N].astype(BF16)
    dt_ref[...] = proj[RIM:, inner + 2 * N : inner + NBC].astype(BF16)


def conv_kernel(pairs, x_ref, bc_ref, dtall_ref, pick_ref, segs_ref, tx_ref, bx_ref, tbc_ref, bbc_ref,
                dtb_ref, alog_ref, dskip_ref, xs_ref, b_ref, c_ref, cum_ref, dto_ref, cumr_ref, dtr_ref,
                raw_ref, run_ref, fresh_ref, fresh16_ref, marks_ref, skip_ref):
    segs = segs_ref[...]
    rows = segs.shape[1]
    same = jnp.where(segs[1:9] == segs[0:1], 1.0, 0.0)
    marks = jnp.concatenate([same, segs[0:8], jnp.zeros((PAIR - 16, rows), F32)], axis=0).T
    marks_ref[...] = marks[:, :16]
    heads = pick_ref.shape[0]
    spread = (
        lax.broadcasted_iota(jnp.int32, (heads, pairs * PAIR), 1) // P_SIZE
        == lax.broadcasted_iota(jnp.int32, (heads, pairs * PAIR), 0)
    ).astype(F32)
    skip_ref[...] = mul(dskip_ref[...], spread, precision=EXACT)
    pre = conv_pre(bc_ref[...].astype(F32), tbc_ref[...], bbc_ref[...], marks)
    act = (pre * jax.nn.sigmoid(pre)).astype(BF16)
    b_rows = act[:, :N]
    b_ref[...] = b_rows
    c_ref[...] = act[:, N:]
    dt_raw = mul(dtall_ref[...], pick_ref[...], NT)
    raw_ref[...] = dt_raw
    raw = dt_raw + dtb_ref[...]
    dt = jnp.maximum(raw, 0.0) + jnp.log1p(jnp.exp(-jnp.abs(raw)))
    cum = mul(tri(rows), dt * -jnp.exp(alog_ref[...]), precision=EXACT)
    cum_ref[...] = cum
    dto_ref[...] = dt
    wide = jnp.concatenate([cum, dt, jnp.zeros((rows, PAIR - 2 * heads), F32)], axis=1)
    turned = wide.T
    cumr_ref[...] = turned[:heads]
    dtr_ref[...] = turned[heads : 2 * heads]
    for p in range(pairs):
        lanes = slice(p * PAIR, (p + 1) * PAIR)
        pre = conv_pre(x_ref[:, lanes].astype(F32), tx_ref[:, lanes], bx_ref[:, lanes], marks)
        act = (pre * jax.nn.sigmoid(pre)).astype(BF16)
        xs_ref[:, lanes] = act
        entry, tail = gains(cum, dt, marks, 2 * p)
        run_ref[:, lanes] = entry[rows - 1 :]
        fresh = mul(b_rows, (tail * act.astype(F32)).astype(BF16), TN)
        fresh_ref[:, lanes] = fresh
        fresh16_ref[:, lanes] = fresh.astype(BF16)


def gate_in_kernel(place_ref, n_ref, cot_ref, *refs):
    z_ref, do_ref = refs[-2:]
    weights = refs[:-2]
    inner = z_ref.shape[1]
    place = place_ref[0]
    z = 0.0
    d_out = 0.0
    for j in range(4):
        z = z + mul(block_lanes(n_ref, place, j), both_halves(weights, j, slice(0, inner)))
        d_out = d_out + mul(
            block_lanes(cot_ref, place, j), both_halves(weights, j, slice(inner, 2 * inner))
        )
    z_ref[...] = z.astype(BF16)
    do_ref[...] = d_out


def output_kernel(seqs, place_ref, *refs):
    normal, d_z, weights = refs[:seqs], refs[seqs : 2 * seqs], refs[2 * seqs : -2]
    mixed_ref, byz_ref = refs[-2:]
    inner = normal[0].shape[1]
    quarter = mixed_ref.shape[2] // 4
    place = place_ref[0]
    for j in range(4):
        here = pl.ds(pl.multiple_of(jnp.bitwise_xor(place, j) * quarter, quarter), quarter)
        w = both_halves(weights, j)
        for b in range(seqs):
            byz_ref[b, :, here] = mul(d_z[b][...], w[:, :inner], NT)
            mixed_ref[b, :, here] = mul(normal[b][...], w[:, inner:], NT)


def block_out_kernel(hid_ref, mine_ref, other_ref, out_ref):
    out_ref[...] = (hid_ref[...].astype(F32) + (mine_ref[...] + other_ref[...])).astype(BF16)


def input_back_kernel(seqs, head_count, place_ref, *refs):
    d_xb, byz_ref, weights, out_ref = refs[:seqs], refs[seqs], refs[seqs + 1 : -1], refs[-1]
    inner = d_xb[0].shape[1] - TAIL
    quarter = out_ref.shape[2] // 4
    place = place_ref[0]
    for j in range(4):
        here = pl.ds(pl.multiple_of(jnp.bitwise_xor(place, j) * quarter, quarter), quarter)
        w = both_halves(weights, j)
        for b in range(seqs):
            out_ref[b, :, here] = (
                byz_ref[b, :, here]
                + mul(d_xb[b][:, :inner], w[:, :inner], NT)
                + mul(d_xb[b][:, inner:], w[:, inner:], NT) / head_count
            )


def weight_grad_kernel(count, seqs, place_ref, *refs):
    lefts, rights = refs[:count], refs[count : count + count * seqs]
    own_ref, low_ref, high_ref, one_ref, two_ref = refs[count + count * seqs :]
    half = own_ref.shape[0] // 2
    quarter = own_ref.shape[0]
    place = place_ref[0]
    start = 0
    for i, left in enumerate(lefts):
        wide = rights[i * seqs].shape[1]
        cols = slice(start, start + wide)
        start += wide
        for j in (1, 3, 2, 0):
            here = pl.ds(pl.multiple_of(jnp.bitwise_xor(place, j) * quarter, quarter), quarter)
            g = 0.0
            for b in range(seqs):
                g = g + mul(left[b, :, here], rights[i * seqs + b][...], TN)
            low, high = g[:half], g[half:]
            if j == 0:
                own_ref[:, cols] = g
            elif j == 1:
                one_ref[:half, cols] = low.astype(BF16)
                high_ref[:, cols] = high
            elif j == 2:
                two_ref[:half, cols] = high.astype(BF16)
                low_ref[:, cols] = low
            else:
                one_ref[half:, cols] = low.astype(BF16)
                two_ref[half:, cols] = high.astype(BF16)


def quarters_kernel(place_ref, own_ref, low_one, low_two, high_two, high_one, own_q, q1, q2, q3, sum_ref):
    half = own_ref.shape[0] // 2
    quarter = own_ref.shape[0] // 4
    sum_ref[:half] = own_ref[:half] + low_one[:half].astype(F32) + low_two[...].astype(F32)
    sum_ref[half:] = own_ref[half:] + high_two[:half].astype(F32) + high_one[...].astype(F32)
    place = place_ref[1]
    for j, ref in enumerate((own_q, q1, q2, q3)):
        here = pl.ds(pl.multiple_of(jnp.bitwise_xor(place, j) * quarter, quarter), quarter)
        ref[...] = sum_ref[here, :].astype(ref.dtype)


def rows_in_order(place, parts, into):
    quarter = parts[0].shape[0]
    for j, part in enumerate(parts):
        here = pl.ds(pl.multiple_of(jnp.bitwise_xor(place, j) * quarter, quarter), quarter)
        into[here, :] = part[...].astype(F32)


def finish_zo_kernel(place_ref, p0, p1, p2, p3, z_ref, o_ref, sum_ref):
    rows_in_order(place_ref[1], (p0, p1, p2, p3), sum_ref)
    inner = z_ref.shape[1]
    z_ref[...] = sum_ref[:, :inner]
    o_ref[...] = sum_ref[:, inner:].T


def finish_x_kernel(place_ref, z_ref, p0, p1, p2, p3, zx_ref, bc_ref, sum_ref):
    inner = z_ref.shape[1]
    rows_in_order(place_ref[1], (p0, p1, p2, p3), sum_ref)
    zx_ref[:, 0, :] = z_ref[...]
    zx_ref[:, 1, :] = sum_ref[:, :inner]
    bc_ref[...] = sum_ref[:, inner:].T[:NBC]


def hidden_back_kernel(mine_ref, other_ref, hid_ref, inv_ref, gain_ref, cot_ref, out_ref, gn_ref):
    d_normed = mine_ref[...] + other_ref[...]
    hid = hid_ref[...].astype(F32)
    inv = inv_ref[...]
    scaled = hid * inv
    gn_ref[...] = jnp.sum(d_normed * scaled, axis=0, keepdims=True)
    q = d_normed * gain_ref[...]
    mean = jnp.sum(q * scaled, axis=1, keepdims=True) / hid.shape[1]
    out_ref[...] = cot_ref[...].astype(F32) + inv * (q - scaled * mean)


def masks_of(seg_col, seg_row):
    rows = seg_col.shape[0]
    t = lax.broadcasted_iota(jnp.int32, (rows, rows), 0)
    s = lax.broadcasted_iota(jnp.int32, (rows, rows), 1)
    return jnp.where((t >= s) & (seg_col == seg_row), 0.0, -1e30).astype(F32)


def block_kernel(heads, x_ref, b_ref, c_ref, cum_ref, cumr_ref, dtr_ref, marks_ref, segs_ref, y_ref,
                 cb_ref, bias_ref):
    cb_ref[...] = mul(c_ref[...], b_ref[...], NT)
    bias_ref[...] = masks_of(marks_ref[:, 8:9], segs_ref[0:1])
    for h in range(0, heads, 2):
        lanes = slice(h * P_SIZE, h * P_SIZE + PAIR)
        parts = []
        for head in (h, h + 1):
            steps = decay_steps(cum_ref[...], cumr_ref[...], dtr_ref[...], bias_ref[...], head)
            parts.append(mul((steps * cb_ref[...]).astype(BF16), x_ref[:, lanes]))
        y_ref[:, lanes] = two(*parts)


def gate_kernel(pairs, yb_ref, x_ref, c_ref, cum_ref, marks_ref, z_ref, do_ref, skip_ref,
                gain_ref, s_ref, y_ref, sums_ref):
    cum = cum_ref[...]
    marks = marks_ref[...]
    square = jnp.zeros((cum.shape[0], PAIR), F32)
    cross = square
    for p in range(pairs):
        lanes = slice(p * PAIR, (p + 1) * PAIR)
        entry = marks[:, 6:7] * jnp.exp(pair_of(cum, 2 * p))
        y_ssd = yb_ref[:, lanes] + entry * mul(c_ref[...], s_ref[:, lanes])
        y_ref[:, lanes] = y_ssd
        y = y_ssd + skip_ref[:, lanes] * x_ref[:, lanes].astype(F32)
        z = z_ref[:, lanes].astype(F32)
        gated = y * z * jax.nn.sigmoid(z)
        square = square + gated * gated
        cross = cross + gated * (do_ref[:, lanes] * gain_ref[:, lanes])
    lane = lax.broadcasted_iota(jnp.int32, (1, 2), 1)
    sums_ref[...] = jnp.where(
        lane == 0,
        jnp.sum(square, axis=1, keepdims=True),
        jnp.sum(cross, axis=1, keepdims=True),
    )


def norm_kernel(pairs, inner_full, y_ref, x_ref, c_ref, cum_ref, marks_ref, z_ref, do_ref, skip_ref,
                gain_ref, sums_ref, on_ref, dy_ref, dz_ref, gg_ref, back_ref, back16_ref):
    cum = cum_ref[...]
    marks = marks_ref[...]
    rms = lax.rsqrt(sums_ref[:, 0:1] / inner_full + EPS)
    coef = rms * rms * sums_ref[:, 1:2] / inner_full
    for p in range(pairs):
        lanes = slice(p * PAIR, (p + 1) * PAIR)
        y = y_ref[:, lanes] + skip_ref[:, lanes] * x_ref[:, lanes].astype(F32)
        z = z_ref[:, lanes].astype(F32)
        sig = jax.nn.sigmoid(z)
        silu = z * sig
        normal = y * silu * rms
        d_out = do_ref[:, lanes]
        on_ref[:, lanes] = (normal * gain_ref[:, lanes]).astype(BF16)
        gg_ref[:, lanes] = jnp.sum(d_out * normal, axis=0, keepdims=True)
        d_gated = d_out * gain_ref[:, lanes] * rms - normal * coef
        d_y = (d_gated * silu).astype(BF16)
        dy_ref[:, lanes] = d_y
        dz_ref[:, lanes] = (d_gated * y * sig * (1.0 + z * (1.0 - sig))).astype(BF16)
        entry = marks[:, 6:7] * jnp.exp(pair_of(cum, 2 * p))
        back = mul(c_ref[...], (entry * d_y.astype(F32)).astype(BF16), TN)
        back_ref[:, lanes] = back
        back16_ref[:, lanes] = back.astype(BF16)


def block_back_kernel(heads, dy_ref, x_ref, b_ref, c_ref, cum_ref, cumr_ref, dtr_ref, marks_ref,
                      segs_ref, back_ref, db_ref, dc_ref, cb_ref, bias_ref, dcb_ref):
    cb_ref[...] = mul(c_ref[...], b_ref[...], NT)
    bias_ref[...] = masks_of(marks_ref[:, 8:9], segs_ref[0:1])
    lane = lax.broadcasted_iota(jnp.int32, (1, PAIR), 1)
    for h in range(0, heads, 2):
        lanes = slice(h * P_SIZE, h * P_SIZE + PAIR)
        d_y = dy_ref[:, lanes]
        x = x_ref[:, lanes]
        parts = []
        for head in (h, h + 1):
            steps = decay_steps(cum_ref[...], cumr_ref[...], dtr_ref[...], bias_ref[...], head)
            mix = (steps * cb_ref[...]).astype(BF16)
            own = (lane < P_SIZE) == (head == h)
            both = mul(jnp.where(own, d_y, jnp.zeros_like(d_y)), x, NT) * steps
            if head == 0:
                dcb_ref[...] = both
            else:
                dcb_ref[...] += both
            parts.append(mul(mix, d_y, TN))
        back_ref[:, lanes] = two(*parts)
    d_cb = dcb_ref[...].astype(BF16)
    dc_ref[...] = mul(d_cb, b_ref[...])
    db_ref[...] = mul(d_cb, c_ref[...], TN)


def state_back_kernel(heads, dy_ref, x_ref, b_ref, c_ref, cum_ref, dt_ref, marks_ref,
                      ub_ref, y_ref, db0_ref, dc0_ref, ext_ref, bcext_ref, tx_ref, bx_ref, tbc_ref,
                      bbc_ref, skip_ref, raw_ref, dtb_ref, alog_ref, pick_ref, g_ref, s_ref,
                      dpre_ref, shared_ref, small_ref, skipg_ref, rim_ref, rimbc_ref, in_ref,
                      out_ref, x_sum_ref, thr_ref):
    cum = cum_ref[...]
    dt = dt_ref[...]
    marks = marks_ref[...]
    rows = cum.shape[0]
    d_b = db0_ref[...]
    d_c = dc0_ref[...]
    for h in range(0, heads, 2):
        lanes = slice(h * P_SIZE, h * P_SIZE + PAIR)
        entry, tail = gains(cum, dt, marks, h)
        d_y16 = dy_ref[:, lanes]
        d_y = d_y16.astype(F32)
        x = x_ref[:, lanes].astype(F32)
        g = g_ref[:, lanes]
        s = s_ref[:, lanes]
        from_state = tail * mul(b_ref[...], g)
        ub = ub_ref[:, lanes]
        d_xs = skip_ref[:, lanes] * d_y + ub + from_state
        d_b = d_b + mul((tail * x).astype(BF16), g, NT)
        d_c = d_c + mul((entry * d_y).astype(BF16), s, NT)
        head_of = lax.broadcasted_iota(jnp.int32, (PAIR, heads), 0) // P_SIZE + h
        pick = (head_of == lax.broadcasted_iota(jnp.int32, (PAIR, heads), 1)).astype(BF16)

        def per_head(v):
            high = v.astype(BF16)
            low = (v - high.astype(F32)).astype(BF16)
            return mul(high, pick) + mul(low, pick)

        inside = per_head(d_y * y_ref[:, lanes] - x * ub)
        outside = per_head(x * from_state)
        along_x = per_head(x * ub)
        if h == 0:
            in_ref[...] = inside
            out_ref[...] = outside
            x_sum_ref[...] = along_x
        else:
            in_ref[...] += inside
            out_ref[...] += outside
            x_sum_ref[...] += along_x
        skipg_ref[:, lanes] = jnp.sum(d_y * x, axis=0, keepdims=True)
        both = per_head(jnp.sum(g.astype(F32) * s.astype(F32), axis=0, keepdims=True))
        if h == 0:
            thr_ref[...] = both
        else:
            thr_ref[...] += both
        pre = conv_pre(ext_ref[:, lanes].astype(F32), tx_ref[:, lanes], bx_ref[:, lanes], marks)
        sig = jax.nn.sigmoid(pre)
        d_pre = d_xs * sig * (1.0 + pre * (1.0 - sig))
        dpre_ref[:, lanes] = d_pre
        rim_ref[:, lanes] = d_pre[:8]
    last = cum[rows - 1 : rows]
    run_gain = marks[rows - 1 : rows, 6:7] * jnp.exp(last)
    through = run_gain * thr_ref[...]
    d_decay = (
        mul(tri(rows, upper=True), in_ref[...], precision=EXACT)
        + mul(tri(rows, strict=True), out_ref[...], precision=EXACT)
        + through
    )
    dt_in = raw_ref[...] + dtb_ref[...]
    sig = jax.nn.sigmoid(dt_in)
    ratio = jnp.where(dt_in < -20.0, 1.0, sig / jnp.maximum(dt, 1e-30))
    d_raw = (x_sum_ref[...] + out_ref[...]) * ratio - jnp.exp(alog_ref[...]) * d_decay * sig
    high = d_raw.astype(BF16)
    low = (d_raw - high.astype(F32)).astype(BF16)
    shared_ref[:, 2 * N :] = jnp.zeros((rows, TAIL - 2 * N), F32)
    shared_ref[:, 2 * N : NBC] = mul(high, pick_ref[...]) + mul(low, pick_ref[...])
    small_ref[...] = jnp.zeros(small_ref.shape, F32)
    small_ref[0:1, :heads] = jnp.sum(d_raw, axis=0, keepdims=True)
    small_ref[1:2, :heads] = -jnp.exp(alog_ref[...]) * jnp.sum(dt * d_decay, axis=0, keepdims=True)
    shared_ref[:, :N] = d_b
    shared_ref[:, N : 2 * N] = d_c
    pre = conv_pre(bcext_ref[...].astype(F32), tbc_ref[...], bbc_ref[...], marks)
    sig = jax.nn.sigmoid(pre)
    slope = sig * (1.0 + pre * (1.0 - sig))
    inner = heads * P_SIZE
    rimbc_ref[:, :N] = d_b[:8] * slope[:8, :N]
    rimbc_ref[:, N:] = d_c[:8] * slope[:8, N:]
    rim_ref[:, inner:] = rimbc_ref[...]


def taps_back(d_pre, rim, ext, taps, marks, dv_ref, lanes, grads_ref):
    rows = d_pre.shape[0]
    longer = jnp.concatenate([d_pre, rim], axis=0)
    d_v = taps[KC - 1 : KC] * d_pre
    for shift in range(1, KC):
        moved = pltpu.roll(longer, rows + 8 - shift, 0)[:rows]
        d_v = d_v + taps[KC - 1 - shift : KC - shift] * moved * marks[:, 2 + shift : 3 + shift]
    dv_ref[:, lanes] = d_v.astype(BF16)
    for k in range(KC):
        v = ext[RIM:] if k == KC - 1 else (
            pltpu.roll(ext, KC - 1 - k, 0)[RIM:] * marks[:, k : k + 1]
        )
        grads_ref[k : k + 1, lanes] = jnp.sum(d_pre * v, axis=0, keepdims=True)
    grads_ref[KC : KC + 1, lanes] = jnp.sum(d_pre, axis=0, keepdims=True)


def conv_back_kernel(pairs, dpre_ref, rim_ref, ext_ref, tx_ref, marks_ref, mine_ref, other_ref,
                     rimbc_ref, bcext_ref, tbc_ref, bbc_ref, dx_ref, grads_ref):
    inner = pairs * PAIR
    marks = marks_ref[...]
    for p in range(pairs):
        lanes = slice(p * PAIR, (p + 1) * PAIR)
        taps_back(dpre_ref[:, lanes], rim_ref[:, lanes], ext_ref[:, lanes].astype(F32),
                  tx_ref[:, lanes], marks, dx_ref, lanes, grads_ref)
    ext = bcext_ref[...].astype(F32)
    pre = conv_pre(ext, tbc_ref[...], bbc_ref[...], marks)
    sig = jax.nn.sigmoid(pre)
    shared = mine_ref[...] + other_ref[...]
    d_pre = shared[:, : 2 * N] * sig * (1.0 + pre * (1.0 - sig))
    taps_back(d_pre, rim_ref[:, inner:] + rimbc_ref[...], ext, tbc_ref[...], marks, dx_ref,
              slice(inner, inner + 2 * N), grads_ref)
    dx_ref[:, inner + 2 * N :] = shared[:, 2 * N :].astype(BF16)


def smalls_kernel(seqs, norm_ref, *refs):
    out_ref = refs[-1]
    conv, head, skip, gate = (refs[i * seqs : (i + 1) * seqs] for i in range(4))
    inner = skip[0].shape[1]

    def total(parts):
        return functools.reduce(lambda a, b: a + b, [p[...] for p in parts])

    out_ref[KC + 1 :] = jnp.zeros((8 - KC - 1, out_ref.shape[1]), F32)
    out_ref[: KC + 1] = total(conv)[: KC + 1]
    out_ref[5:6, :inner] = jnp.sum(norm_ref[...], axis=0)
    out_ref[6:7, :inner] = total(gate)
    out_ref[7:8, :inner] = total(skip)
    both = total(head)
    out_ref[5:6, inner : inner + PAIR] = both[0:1]
    out_ref[6:7, inner : inner + PAIR] = both[1:2]


def smalls_out_kernel(all_ref, gn_ref, tx_ref, bx_ref, tbc_ref, bbc_ref, dtb_ref, alog_ref, skip_ref,
                      gg_ref):
    inner = gn_ref.shape[1]
    heads = dtb_ref.shape[1]
    tx_ref[...] = all_ref[:KC, :inner]
    tbc_ref[...] = all_ref[:KC, inner:]
    bx_ref[...] = all_ref[KC : KC + 1, :inner]
    bbc_ref[...] = all_ref[KC : KC + 1, inner:]
    gn_ref[...] = all_ref[5:6, :inner]
    gg_ref[...] = all_ref[6:7, :inner]
    dtb_ref[...] = all_ref[5:6, inner : inner + heads]
    alog_ref[...] = all_ref[6:7, inner : inner + heads]
    lane = lax.broadcasted_iota(jnp.int32, (inner, heads), 0) // P_SIZE
    pick = (lane == lax.broadcasted_iota(jnp.int32, (inner, heads), 1)).astype(F32)
    skip_ref[...] = mul(all_ref[7:8, :inner], pick, precision=EXACT)


def launch(order, kernel, name, ins, outs, scratch=(), grid=(1,)):
    def spec(block, index):
        if block is None:
            return pl.BlockSpec(memory_space=pltpu.SMEM)
        return pl.BlockSpec(block, index)

    values = [a for a, _, _ in ins]
    if order is not None:
        values = order.after(*values)
    results = pl.pallas_call(
        kernel,
        grid=grid,
        in_specs=[spec(block, index) for _, block, index in ins],
        out_specs=[spec(block, index) for _, block, index in outs],
        out_shape=[jax.ShapeDtypeStruct(*form) for form, _, _ in outs],
        scratch_shapes=list(scratch),
        compiler_params=pltpu.CompilerParams(vmem_limit_bytes=VMEM),
        name=name,
    )(*values)
    if order is not None:
        order.did(results[0])
    return results


def at(a, b):
    return a, (None,) + a.shape[1:], lambda *_: (b,) + (0,) * (a.ndim - 1)


def own(a):
    return a, (None,) + a.shape[1:], lambda b: (b,) + (0,) * (a.ndim - 1)


def every(a):
    a = a.reshape((1, -1)) if a.ndim == 1 else a
    return a, a.shape, lambda *b: (0,) * a.ndim


def scalar(a):
    return a, None, None


def gives_whole(shape, kind):
    return (shape, kind), shape, lambda *b: (0,) * len(shape)


def head_parts(value):
    if lax.axis_size("head") == 2:
        return value, hop(value, "head", 1)
    return lax.psum(value, "head"), jnp.zeros_like(value)


def grads_begin(order, place, lefts, rights):
    wide = sum(r[0].shape[1] for r in rights)
    quarter = lefts[0].shape[2] // lax.axis_size("fsdp")
    half = quarter // 2
    return launch(
        order,
        functools.partial(weight_grad_kernel, len(lefts), len(rights[0])),
        "weight_grad",
        [scalar(place)] + [every(a) for a in lefts] + [every(a) for r in rights for a in r],
        [
            gives_whole((quarter, wide), F32),
            gives_whole((half, wide), F32),
            gives_whole((half, wide), F32),
            gives_whole((quarter, wide), BF16),
            gives_whole((quarter, wide), BF16),
        ],
    )


def grads_first(terms):
    _, _, _, one, two_way = terms
    return hop(one, "fsdp", 1), hop(two_way, "fsdp", 2)


def grads_second(order, terms, first):
    _, low, high, _, _ = terms
    half = low.shape[0]
    low_one, high_two = order.after(*first)
    low_next = (low + low_one[half:].astype(F32)).astype(BF16)
    high_next = (high + high_two[half:].astype(F32)).astype(BF16)
    order.did(high_next)
    return hop(low_next, "fsdp", 2), hop(high_next, "fsdp", 1)


def grads_quarters(order, place, terms, first, second):
    mine = terms[0]
    quarter = (mine.shape[0] // 4, mine.shape[1])
    return launch(
        order,
        quarters_kernel,
        "quarters",
        [scalar(place)] + [every(a) for a in (mine, first[0], second[0], first[1], second[1])],
        [gives_whole(quarter, F32)] + [gives_whole(quarter, BF16)] * 3,
        [pltpu.VMEM(mine.shape, F32)],
    )


def line_terms(quarters):
    return [hop(q, "seq", j) for j, q in enumerate(quarters[1:], 1)]


def line_sum(order, mine, terms):
    total = mine
    for term in order.after(*terms):
        total = total + term.astype(F32)
    return order.did(total.astype(BF16))


def line_parts(total):
    return [total] + [hop(total, "seq", j) for j in range(1, 4)]


def shards(
    hidden,
    segment_ids,
    norm_gain,
    w_zx,
    w_bcdt,
    conv_x,
    conv_x_bias,
    conv_bc,
    conv_bc_bias,
    dt_bias,
    a_log,
    d_skip,
    gate_gain,
    w_out,
    cotangent,
):
    head_place = lax.axis_index("head")
    head_count = lax.axis_size("head")
    seq_place = lax.axis_index("seq")
    seq_count = lax.axis_size("seq")
    place = jnp.stack([lax.axis_index("fsdp"), seq_place]).astype(jnp.int32)
    by_blocks = square("fsdp") and square("seq")
    seqs, rows, width = hidden.shape
    own_rows, _, inner = w_zx.shape
    heads = dt_bias.shape[0]
    inner_full = inner * head_count
    longer = rows + RIM
    pairs = heads // 2
    wide_x = inner + TAIL
    each = range(seqs)

    def gives(shape, kind):
        return ((seqs,) + shape, kind), (None,) + shape, lambda b: (b,) + (0,) * len(shape)

    order = Order()

    if by_blocks:
        half = own_rows // 2
        x_low, x_high = launch(
            order,
            pack_x_kernel,
            "pack_x",
            [every(w_zx), every(w_bcdt.T)],
            [gives_whole((half, wide_x), BF16)] * 2,
        )
        w_x = gather_halves(x_low, x_high, "fsdp")
    else:
        x_own = jnp.concatenate([w_zx[:, 1], jnp.pad(w_bcdt, ((0, 0), (0, TAIL - NBC)))], axis=1)
        w_x = lax.all_gather(x_own, "fsdp", axis=0, tiled=True)
        zo_own = jnp.concatenate([w_zx[:, 0], w_out.T], axis=1)
        w_zo = lax.all_gather(zo_own, "fsdp", axis=0, tiled=True)

    def input_norm(part):
        part = part.astype(F32)
        inv = lax.rsqrt(jnp.mean(part * part, axis=-1, keepdims=True) + EPS)
        return (part * inv * norm_gain).astype(BF16), inv

    before = step_along(hidden[:, rows - RIM :], "seq", 1)
    normed, inv_rms = input_norm(hidden)

    edge = KC - 1
    seg_ids = segment_ids if not by_blocks else tie(segment_ids, w_x[2], w_x[5])
    seg_padded = jnp.pad(seg_ids, ((0, 0), (edge, 0)), constant_values=-1)
    seg_padded = jnp.pad(seg_padded, ((0, 0), (0, edge)), constant_values=-2)
    seg_wide = lax.dynamic_slice_in_dim(seg_padded, seq_place * rows, rows + 2 * edge, 1).astype(F32)
    seg = seg_wide[:, edge : edge + rows]
    near = [seg] + [seg_wide[:, k : k + rows] for k in range(edge)]
    near += [seg_wide[:, edge + k : edge + k + rows] for k in range(1, KC)]
    near += [jnp.broadcast_to(s, seg.shape) for s in (seg_wide[:, edge - 1 : edge], seg[:, -1:])]
    segs = jnp.pad(jnp.stack(near, axis=1), ((0, 0), (0, 16 - len(near)), (0, 0)))
    head_pick = (
        jnp.arange(heads)[:, None] + head_place * heads == jnp.arange(NH)[None, :]
    ).astype(BF16)
    normed_rim, _ = input_norm(before)

    if by_blocks:
        zo_low, zo_high = launch(
            order,
            pack_zo_kernel,
            "pack_zo",
            [every(w_zx), every(w_out)],
            [gives_whole((half, 2 * inner), BF16)] * 2,
        )

    def project(b):
        if by_blocks:
            return launch(
                order,
                input_kernel,
                "input",
                [scalar(place), at(normed_rim, b), at(normed, b)] + [every(w) for w in w_x],
                [
                    gives_whole((longer, inner), BF16),
                    gives_whole((longer, 2 * N), BF16),
                    gives_whole((rows, NH), BF16),
                ],
            )
        proj = jnp.dot(
            jnp.concatenate([normed_rim[b], normed[b]], axis=0), w_x, preferred_element_type=F32
        ).astype(BF16)
        return (
            proj[:, :inner],
            proj[:, inner : inner + 2 * N],
            proj[RIM:, inner + 2 * N : inner + NBC],
        )

    conv_params = [every(conv_x), every(conv_x_bias), every(conv_bc), every(conv_bc_bias)]

    def convolve(b, x_ext, bc_ext, dt_all):
        return launch(
            order,
            functools.partial(conv_kernel, pairs),
            "conv",
            [every(x_ext), every(bc_ext), every(dt_all), every(head_pick), at(segs, b)]
            + conv_params
            + [every(dt_bias), every(a_log), every(d_skip)],
            [
                gives_whole((rows, inner), BF16),
                gives_whole((rows, N), BF16),
                gives_whole((rows, N), BF16),
                gives_whole((rows, heads), F32),
                gives_whole((rows, heads), F32),
                gives_whole((heads, rows), F32),
                gives_whole((heads, rows), F32),
                gives_whole((rows, heads), F32),
                gives_whole((1, inner), F32),
                gives_whole((N, inner), F32),
                gives_whole((N, inner), BF16),
                gives_whole((rows, 16), F32),
                gives_whole((1, inner), F32),
            ],
        )

    def depart(sent, steps):
        return step_along(sent, "seq", steps)

    def onward(entering, own_state, gain, steps):
        (entering,) = order.after(entering)
        leaving = order.did((gain * entering.astype(F32) + own_state).astype(BF16))
        return step_along(leaving, "seq", steps)

    ext = []
    parts = []
    moving = []
    for b in each:
        ext.append(project(b))
        parts.append(convolve(b, *ext[b]))
        moving.append(depart(parts[b][10], 1))
    xs, bs, cs, cum, dt, cum_rows, dt_rows, raw, run_gain, fresh, _, marks, skips = zip(*parts)
    skip = skips[0]

    square_form = pltpu.VMEM((rows, rows), F32)

    def block(b):
        return launch(
            order,
            functools.partial(block_kernel, heads),
            "block",
            [every(a[b]) for a in (xs, bs, cs, cum, cum_rows, dt_rows, marks)] + [at(segs, b)],
            [gives_whole((rows, inner), F32)],
            [square_form] * 2,
        )[0]

    if by_blocks:
        zo_low, zo_high = order.after(zo_low, zo_high)
        w_zo = gather_halves(zo_low, zo_high, "fsdp")
    y_block = [block(b) for b in each]
    laps = max(0, seq_count - 2)
    for lap in range(laps):
        moving = [onward(moving[b], fresh[b], run_gain[b], 1) for b in each]
        if lap > 0 or laps == 1:
            continue
    state_in = moving if seq_count > 1 else [jnp.zeros_like(m) for m in moving]

    if by_blocks:
        z, d_outn = launch(
            order,
            gate_in_kernel,
            "gate_in",
            [scalar(place), own(normed), own(cotangent)] + [every(w) for w in w_zo],
            [gives((rows, inner), BF16), gives((rows, inner), F32)],
            grid=(seqs,),
        )
    else:
        z = jnp.dot(normed, w_zo[:, :inner], preferred_element_type=F32).astype(BF16)
        d_outn = jnp.dot(cotangent, w_zo[:, inner:], preferred_element_type=F32)

    def gate(b):
        y_ssd, sums = launch(
            order,
            functools.partial(gate_kernel, pairs),
            "gate",
            [every(a[b]) for a in (y_block, xs, cs, cum, marks)]
            + [at(a, b) for a in (z, d_outn)]
            + [every(skip), every(gate_gain), every(state_in[b])],
            [gives_whole((rows, inner), F32), gives_whole((rows, 2), F32)],
        )
        return y_ssd, sum_all(sums, ("head",))

    def norm(b, y_ssd, sums):
        return launch(
            order,
            functools.partial(norm_kernel, pairs, inner_full),
            "norm",
            [every(a) for a in (y_ssd, xs[b], cs[b], cum[b], marks[b])]
            + [at(a, b) for a in (z, d_outn)]
            + [every(skip), every(gate_gain), every(sums)],
            [
                gives_whole((rows, inner), BF16),
                gives_whole((rows, inner), BF16),
                gives_whole((rows, inner), BF16),
                gives_whole((1, inner), F32),
                gives_whole((N, inner), F32),
                gives_whole((N, inner), BF16),
            ],
        )

    y_ssd = []
    normals = []
    moving = []
    for b in each:
        y_b, sums = gate(b)
        y_ssd.append(y_b)
        normals.append(norm(b, y_b, sums))
        moving.append(depart(normals[b][5], -1))
    out_norm, d_y, d_z, grad_gate, back, _ = zip(*normals)

    if by_blocks:
        zo_terms = grads_begin(order, place, [normed, cotangent], [d_z, out_norm])
        zo_first = grads_first(zo_terms)

    def block_back(b):
        return launch(
            order,
            functools.partial(block_back_kernel, heads),
            "block_back",
            [every(a[b]) for a in (d_y, xs, bs, cs, cum, cum_rows, dt_rows, marks)] + [at(segs, b)],
            [
                gives_whole((rows, inner), F32),
                gives_whole((rows, N), F32),
                gives_whole((rows, N), F32),
            ],
            [square_form] * 3,
        )

    def back_lap():
        return [onward(moving[b], back[b], run_gain[b], -1) for b in each]

    block_parts = [block_back(0)]
    if laps > 0:
        moving = back_lap()
    block_parts += [block_back(b) for b in each[1:]]

    if by_blocks:
        mixed, by_z = launch(
            order,
            functools.partial(output_kernel, seqs),
            "output",
            [scalar(place)] + [every(a) for a in out_norm + d_z] + [every(w) for w in w_zo],
            [gives_whole((seqs, rows, width), F32)] * 2,
        )
    else:
        last = (((2,), (1,)), ((), ()))
        mixed = mul(jnp.stack(out_norm), w_zo[:, inner:], last)
        by_z = mul(jnp.stack(d_z), w_zo[:, :inner], last)
    mixed, mixed_other = head_parts(mixed)
    for lap in range(1, laps):
        moving = back_lap()
    (block_out,) = launch(
        order,
        block_out_kernel,
        "block_out",
        [every(hidden), every(mixed), every(mixed_other)],
        [gives_whole((seqs, rows, width), BF16)],
    )
    grad_state = moving if seq_count > 1 else [jnp.zeros_like(m) for m in moving]
    back_x, d_b, d_c = zip(*block_parts)

    def state_back(b):
        x_ext, bc_ext, _ = ext[b]
        return launch(
            order,
            functools.partial(state_back_kernel, heads),
            "state_back",
            [every(a[b]) for a in (d_y, xs, bs, cs, cum, dt, marks)]
            + [every(a) for a in (back_x[b], y_ssd[b], d_b[b], d_c[b], x_ext, bc_ext)]
            + conv_params
            + [every(a) for a in (skip, raw[b], dt_bias, a_log, head_pick, grad_state[b], state_in[b])],
            [
                gives_whole((rows, inner), F32),
                gives_whole((rows, TAIL), F32),
                gives_whole((2, PAIR), F32),
                gives_whole((1, inner), F32),
                gives_whole((8, inner + 2 * N), F32),
                gives_whole((8, 2 * N), F32),
            ],
            [pltpu.VMEM((rows, heads), F32)] * 3 + [pltpu.VMEM((1, heads), F32)],
        )

    def neighbours(shared, rim, rim_bc):
        rim_other = jnp.zeros_like(rim_bc)
        for turn in range(1, head_count):
            rim_other = rim_other + lax.ppermute(
                rim_bc,
                ("seq", "head"),
                [
                    (s * head_count + p, (s - 1) * head_count + (p + turn) % head_count)
                    for s in range(1, seq_count)
                    for p in range(head_count)
                ],
            )
        return head_parts(shared) + (step_along(rim, "seq", -1), rim_other)

    def conv_back(b, d_pre, shared, shared_other, rim, rim_other):
        x_ext, bc_ext, _ = ext[b]
        return launch(
            order,
            functools.partial(conv_back_kernel, pairs),
            "conv_back",
            [every(d_pre), every(rim), every(x_ext), every(conv_x), every(marks[b])]
            + [every(a) for a in (shared, shared_other, rim_other, bc_ext, conv_bc, conv_bc_bias)],
            [gives_whole((rows, wide_x), BF16), gives_whole((8, inner + 2 * N), F32)],
        )

    state_parts = []
    near_parts = []
    for b in each:
        state_parts.append(state_back(b))
        _, shared, _, _, rim, rim_bc = state_parts[b]
        near_parts.append(neighbours(shared, rim, rim_bc))
        if by_blocks and b == 0:
            zo_second = grads_second(order, zo_terms, zo_first)
    d_xb, grad_conv = zip(*[conv_back(b, state_parts[b][0], *near_parts[b]) for b in each])
    small = [s[2] for s in state_parts]
    grad_skip = [s[3] for s in state_parts]

    if by_blocks:
        x_terms = grads_begin(order, place, [normed], [d_xb])
        x_first = grads_first(x_terms)
        zo_quarters = grads_quarters(order, place, zo_terms, zo_first, zo_second)
        zo_line = line_terms(zo_quarters)
        (by_head,) = launch(
            order,
            functools.partial(input_back_kernel, seqs, head_count),
            "input_back",
            [scalar(place)] + [every(a) for a in d_xb] + [every(by_z)] + [every(w) for w in w_x],
            [gives_whole((seqs, rows, width), F32)],
        )
    else:
        dxb = jnp.stack(d_xb)
        by_head = (
            by_z
            + mul(dxb[..., :inner], w_x[:, :inner], last)
            + mul(dxb[..., inner:], w_x[:, inner:], last) / head_count
        )
    by_head, by_other = head_parts(by_head)
    grad_hidden, grad_norm = launch(
        order,
        hidden_back_kernel,
        "hidden_back",
        [own(by_head), own(by_other), own(hidden), own(inv_rms), every(norm_gain), own(cotangent)],
        [gives((rows, width), F32), gives((1, width), F32)],
        grid=(seqs,),
    )

    (flat,) = launch(
        order,
        functools.partial(smalls_kernel, seqs),
        "smalls",
        [every(grad_norm)] + [every(a) for part in (grad_conv, small, grad_skip, grad_gate) for a in part],
        [gives_whole((8, inner + 2 * N), F32)],
    )
    flat = sum_all(flat, ("seq",))

    if by_blocks:
        x_second = grads_second(order, x_terms, x_first)
        zo_parts = line_parts(line_sum(order, zo_quarters[0], zo_line))
        x_quarters = grads_quarters(order, place, x_terms, x_first, x_second)
        x_line = line_terms(x_quarters)
        flat = sum_all(flat, ("fsdp",))
        grad_z, grad_o = launch(
            order,
            finish_zo_kernel,
            "finish_zo",
            [scalar(place)] + [every(a) for a in zo_parts],
            [gives_whole((own_rows, inner), F32), gives_whole((inner, own_rows), F32)],
            [pltpu.VMEM((own_rows, 2 * inner), F32)],
        )
        x_parts = line_parts(line_sum(order, x_quarters[0], x_line))
    else:
        flat = sum_all(flat, ("fsdp",))
    grad_norm, grad_tx, grad_bx, grad_tbc, grad_bbc, grad_dtb, grad_alog, grad_skip, grad_gate = launch(
        order,
        smalls_out_kernel,
        "smalls_out",
        [every(flat)],
        [
            gives_whole(shape, F32)
            for shape in (
                (1, width),
                (KC, inner),
                (1, inner),
                (KC, 2 * N),
                (1, 2 * N),
                (1, heads),
                (1, heads),
                (1, heads),
                (1, inner),
            )
        ],
    )
    if by_blocks:
        grad_zx, grad_bcdt = launch(
            order,
            finish_x_kernel,
            "finish_x",
            [scalar(place), every(grad_z)] + [every(a) for a in x_parts],
            [gives_whole((own_rows, 2, inner), F32), gives_whole((NBC, own_rows), F32)],
            [pltpu.VMEM((own_rows, wide_x), F32)],
        )
        grad_bcdt = grad_bcdt.T
    else:
        def owned(left, right):
            full = lax.dot_general(
                left, jnp.stack(right), (((0, 1), (0, 1)), ((), ())), preferred_element_type=F32
            )
            return lax.psum(lax.psum_scatter(full, "fsdp", scatter_dimension=0, tiled=True), "seq")

        grad_x = owned(normed, d_xb)
        grad_zx = jnp.stack([owned(normed, d_z), grad_x[:, :inner]], axis=1)
        grad_bcdt = grad_x[:, inner : inner + NBC]
        grad_o = owned(cotangent, out_norm).T
    return (
        block_out,
        grad_hidden,
        grad_norm.reshape(-1),
        grad_zx,
        grad_bcdt,
        grad_tx,
        grad_bx.reshape(-1),
        grad_tbc,
        grad_bbc.reshape(-1),
        grad_dtb.reshape(-1),
        grad_alog.reshape(-1),
        grad_skip.reshape(-1),
        grad_gate.reshape(-1),
        grad_o,
    )


def solution(mesh):
    placed = (
        P("fsdp", "seq", None),
        P("fsdp", None),
        P(),
        P("fsdp", None, "head"),
        P("fsdp", None),
        P(None, "head"),
        P("head"),
        P(),
        P(),
        P("head"),
        P("head"),
        P("head"),
        P("head"),
        P("head", "fsdp"),
        P("fsdp", "seq", None),
    )
    return jax.shard_map(
        shards,
        mesh=mesh,
        in_specs=placed,
        out_specs=(
            P("fsdp", "seq", None),
            P("fsdp", "seq", None),
            P(),
            P("fsdp", None, "head"),
            P("fsdp", None),
            P(None, "head"),
            P("head"),
            P(),
            P(),
            P("head"),
            P("head"),
            P("head"),
            P("head"),
            P("head", "fsdp"),
        ),
        check_vma=False,
    )
```

```python
import functools

import jax
import jax.numpy as jnp
from jax import lax
from jax.experimental import pallas as pl
from jax.experimental.pallas import tpu as pltpu
from jax.sharding import PartitionSpec as P

P_SIZE = 64
N = 128
NH = 32
KC = 4
NBC = 288
TAIL = 384
RIM = 16
PAIR = 128

EPS = 1e-05
F32 = jnp.float32
BF16 = jnp.bfloat16
EXACT = lax.Precision.HIGHEST
VMEM = 24 * 2**20


def hop(value, axis, bit):
    return lax.ppermute(value, axis, [(i, i ^ bit) for i in range(lax.axis_size(axis))])


def step_along(value, axis, steps):
    count = lax.axis_size(axis)
    initial, last = (max(0, -steps), min(count, count - steps))
    return lax.ppermute(value, axis, [(source, source + steps) for source in range(initial, last)])


class Order:
    def __init__(self):
        self.last = None

    def after(self, *values):
        if self.last is None:
            return values
        return lax.optimization_barrier(values + (self.last,))[:-1]

    def did(self, value):
        self.last = value
        return value


def pass_along(value, axis, lap, steps):
    source = lap if steps > 0 else lax.axis_size(axis) - 1 - lap
    return lax.ppermute(value, axis, [(source, source + steps)])


def square(axis):
    return lax.axis_size(axis) == 4


def tie(value, *others):
    return lax.optimization_barrier((value,) + others)[0]


def gather_halves(order, low, high, axis):
    low_one = hop(low, axis, 1)
    high_two = hop(high, axis, 2)
    high_one = hop(high, axis, 1)
    low_two = hop(low, axis, 2)
    low_one, high_two = order.after(low_one, high_two)
    order.did(low_one)
    low_three = hop(low_one, axis, 2)
    high_three = hop(high_two, axis, 1)
    return [low, high, low_one, high_one, low_two, high_two, low_three, high_three]


def gather_first(both, axis):
    return hop(both, axis, 1), hop(both, axis, 2)


def gather_second(order, both, first, axis):
    half = both.shape[0] // 2
    one, two = order.after(*first)
    order.did(one)
    low_three = hop(one[:half], axis, 2)
    high_three = hop(two[half:], axis, 1)
    return [both, one, two, low_three, high_three]


def sum_all(value, axes):
    for axis in axes:
        count = lax.axis_size(axis)
        if count & (count - 1):
            value = lax.psum(value, axis)
            continue
        bit = 1
        while bit < count:
            value = value + hop(value, axis, bit)
            bit *= 2
    return value


NT = (((1,), (1,)), ((), ()))
TN = (((0,), (0,)), ((), ()))
NN = (((1,), (0,)), ((), ()))


def mul(a, b, dims=NN, precision=None):
    return lax.dot_general(a, b, dims, precision=precision, preferred_element_type=F32)


def tri(rows, strict=False, upper=False):
    t = lax.broadcasted_iota(jnp.int32, (rows, rows), 0)
    s = lax.broadcasted_iota(jnp.int32, (rows, rows), 1)
    if upper:
        t, s = s, t
    return jnp.where(t > s if strict else t >= s, 1.0, 0.0).astype(F32)


def two(left, right):
    lane = lax.broadcasted_iota(jnp.int32, (1, PAIR), 1)
    return jnp.where(lane < P_SIZE, left, right)


def pair_of(columns, head):
    return two(columns[:, head : head + 1], columns[:, head + 1 : head + 2])


def conv_pre(ext, taps, bias, marks):
    pre = bias + taps[KC - 1 : KC] * ext[RIM:]
    for k in range(KC - 1):
        pre = pre + taps[k : k + 1] * pltpu.roll(ext, KC - 1 - k, 0)[RIM:] * marks[:, k : k + 1]
    return pre


def gains(cum, dt, marks, head):
    rows = cum.shape[0]
    cum_pair = pair_of(cum, head)
    last = two(cum[rows - 1 : rows, head : head + 1], cum[rows - 1 : rows, head + 1 : head + 2])
    entry = marks[:, 6:7] * jnp.exp(cum_pair)
    tail = marks[:, 7:8] * jnp.exp(last - cum_pair) * pair_of(dt, head)
    return entry, tail


def decay_steps(cum, cum_rows, dt_rows, bias, head):
    return (
        jnp.exp(cum[:, head : head + 1] - cum_rows[head : head + 1] + bias)
        * dt_rows[head : head + 1]
    )


def block_lanes(ref, place, j):
    width = ref.shape[1] // 4
    return ref[:, pl.ds(pl.multiple_of(jnp.bitwise_xor(place, j) * width, width), width)]


def both_halves(refs, j, lanes=slice(None)):
    if len(refs) == 5 and j < 3:
        return refs[j][:, lanes]
    if len(refs) == 5:
        return jnp.concatenate([refs[3][:, lanes], refs[4][:, lanes]], axis=0)
    return jnp.concatenate([refs[2 * j][:, lanes], refs[2 * j + 1][:, lanes]], axis=0)


def pack_x_kernel(w_ref, bc_ref, low_ref, high_ref):
    half = w_ref.shape[0] // 2
    inner = w_ref.shape[2]
    low_ref[:, :inner] = w_ref[:half, 1, :]
    high_ref[:, :inner] = w_ref[half:, 1, :]
    turned = bc_ref[...].astype(F32).T.astype(BF16)
    for ref, part in ((low_ref, turned[:half]), (high_ref, turned[half:])):
        ref[:, inner + 2 * N :] = jnp.zeros((half, TAIL - 2 * N), BF16)
        ref[:, inner : inner + NBC] = part


def pack_zo_kernel(w_ref, o_ref, out_ref):
    inner = w_ref.shape[2]
    out_ref[:, :inner] = w_ref[:, 0, :]
    out_ref[:, inner:] = o_ref[...].astype(F32).T.astype(BF16)


def input_kernel(place_ref, rim_ref, n_ref, *refs):
    x_ref, bc_ref, dt_ref = refs[-3:]
    weights = refs[:8]
    inner = x_ref.shape[1]
    place = place_ref[0]
    proj = 0.0
    for j in range(4):
        rows = jnp.concatenate([block_lanes(rim_ref, place, j), block_lanes(n_ref, place, j)], axis=0)
        proj = proj + mul(rows, both_halves(weights, j))
    x_ref[...] = proj[:, :inner].astype(BF16)
    bc_ref[...] = proj[:, inner : inner + 2 * N].astype(BF16)
    dt_ref[...] = proj[RIM:, inner + 2 * N : inner + NBC].astype(BF16)


def conv_kernel(pairs, x_ref, bc_ref, dtall_ref, pick_ref, segs_ref, tx_ref, bx_ref, tbc_ref, bbc_ref,
                dtb_ref, alog_ref, dskip_ref, *refs):
    (xs_ref, b_ref, c_ref, cum_ref, dto_ref, cumr_ref, dtr_ref, raw_ref, marks_ref, run_ref,
     fresh_ref, fresh16_ref, skip_ref) = refs[-13:]
    segs = segs_ref[...]
    rows = segs.shape[1]
    same = jnp.where(segs[1:9] == segs[0:1], 1.0, 0.0)
    marks = jnp.concatenate([same, segs[0:8], jnp.zeros((PAIR - 16, rows), F32)], axis=0).T
    marks_ref[...] = marks[:, :16]
    heads = pick_ref.shape[0]
    spread = (
        lax.broadcasted_iota(jnp.int32, (heads, pairs * PAIR), 1) // P_SIZE
        == lax.broadcasted_iota(jnp.int32, (heads, pairs * PAIR), 0)
    ).astype(F32)
    skip_ref[...] = mul(dskip_ref[...], spread, precision=EXACT)
    pre = conv_pre(bc_ref[...].astype(F32), tbc_ref[...], bbc_ref[...], marks)
    act = (pre * jax.nn.sigmoid(pre)).astype(BF16)
    b_rows = act[:, :N]
    b_ref[...] = b_rows
    c_ref[...] = act[:, N:]
    dt_raw = mul(dtall_ref[...], pick_ref[...], NT)
    raw_ref[...] = dt_raw
    raw = dt_raw + dtb_ref[...]
    dt = jnp.maximum(raw, 0.0) + jnp.log1p(jnp.exp(-jnp.abs(raw)))
    cum = mul(tri(rows), dt * -jnp.exp(alog_ref[...]), precision=EXACT)
    cum_ref[...] = cum
    dto_ref[...] = dt
    wide = jnp.concatenate([cum, dt, jnp.zeros((rows, PAIR - 2 * heads), F32)], axis=1)
    turned = wide.T
    cumr_ref[...] = turned[:heads]
    dtr_ref[...] = turned[heads : 2 * heads]
    for p in range(pairs):
        lanes = slice(p * PAIR, (p + 1) * PAIR)
        pre = conv_pre(x_ref[:, lanes].astype(F32), tx_ref[:, lanes], bx_ref[:, lanes], marks)
        act = (pre * jax.nn.sigmoid(pre)).astype(BF16)
        xs_ref[:, lanes] = act
        entry, tail = gains(cum, dt, marks, 2 * p)
        run_ref[:, lanes] = entry[rows - 1 :]
        fresh = mul(b_rows, (tail * act.astype(F32)).astype(BF16), TN)
        fresh_ref[:, lanes] = fresh
        fresh16_ref[:, lanes] = fresh.astype(BF16)


def gate_in_kernel(place_ref, n_ref, cot_ref, *refs):
    z_ref, do_ref = refs[-2:]
    weights = refs[:-2]
    inner = z_ref.shape[1]
    place = place_ref[0]
    z = 0.0
    d_out = 0.0
    for j in range(4):
        z = z + mul(block_lanes(n_ref, place, j), both_halves(weights, j, slice(0, inner)))
        d_out = d_out + mul(
            block_lanes(cot_ref, place, j), both_halves(weights, j, slice(inner, 2 * inner))
        )
    z_ref[...] = z.astype(BF16)
    do_ref[...] = d_out


def output_kernel(place_ref, on_ref, dz_ref, *refs):
    weights = refs[:-2]
    mixed_ref, byz_ref = refs[-2:]
    inner = on_ref.shape[1]
    quarter = mixed_ref.shape[1] // 4
    place = place_ref[0]
    for j in range(4):
        here = pl.ds(pl.multiple_of(jnp.bitwise_xor(place, j) * quarter, quarter), quarter)
        w = both_halves(weights, j)
        byz_ref[:, here] = mul(dz_ref[...], w[:, :inner], NT)
        mixed_ref[:, here] = mul(on_ref[...], w[:, inner:], NT).astype(BF16)


def block_out_kernel(hid_ref, mine_ref, other_ref, out_ref):
    mixed = mine_ref[...].astype(F32) + other_ref[...].astype(F32)
    out_ref[...] = (hid_ref[...].astype(F32) + mixed).astype(BF16)


def input_back_kernel(head_count, place_ref, dxb_ref, byz_ref, *refs):
    weights, out_ref = refs[:-1], refs[-1]
    inner = dxb_ref.shape[1] - TAIL
    quarter = out_ref.shape[1] // 4
    place = place_ref[0]
    for j in range(4):
        here = pl.ds(pl.multiple_of(jnp.bitwise_xor(place, j) * quarter, quarter), quarter)
        w = both_halves(weights, j)
        out_ref[:, here] = (
            byz_ref[:, here]
            + mul(dxb_ref[:, :inner], w[:, :inner], NT)
            + mul(dxb_ref[:, inner:], w[:, inner:], NT) / head_count
        ).astype(BF16)


def weight_grad_kernel(count, seqs, place_ref, *refs):
    lefts, rights = refs[:count], refs[count : 2 * count]
    own_ref, low_ref, high_ref, one_ref, two_ref = refs[2 * count :]
    half = own_ref.shape[0] // 2
    quarter = own_ref.shape[0]
    place = place_ref[0]
    start = 0
    for i, left in enumerate(lefts):
        wide = rights[i].shape[2]
        cols = slice(start, start + wide)
        start += wide
        for j in (1, 3, 2, 0):
            here = pl.ds(pl.multiple_of(jnp.bitwise_xor(place, j) * quarter, quarter), quarter)
            g = 0.0
            for b in range(seqs):
                g = g + mul(left[b, :, here], rights[i][b], TN)
            low, high = g[:half], g[half:]
            if j == 0:
                own_ref[:, cols] = g
            elif j == 1:
                one_ref[:half, cols] = low.astype(BF16)
                high_ref[:, cols] = high
            elif j == 2:
                two_ref[:half, cols] = high.astype(BF16)
                low_ref[:, cols] = low
            else:
                one_ref[half:, cols] = low.astype(BF16)
                two_ref[half:, cols] = high.astype(BF16)


def quarters_kernel(place_ref, own_ref, low_one, low_two, high_two, high_one, own_q, q1, q2, q3, sum_ref):
    half = own_ref.shape[0] // 2
    quarter = own_ref.shape[0] // 4
    sum_ref[:half] = own_ref[:half] + low_one[:half].astype(F32) + low_two[...].astype(F32)
    sum_ref[half:] = own_ref[half:] + high_two[:half].astype(F32) + high_one[...].astype(F32)
    place = place_ref[1]
    for j, ref in enumerate((own_q, q1, q2, q3)):
        here = pl.ds(pl.multiple_of(jnp.bitwise_xor(place, j) * quarter, quarter), quarter)
        ref[...] = sum_ref[here, :].astype(ref.dtype)


def halves_kernel(place_ref, own_ref, low_one, low_two, high_two, high_one, keep_ref, send_ref, sum_ref):
    half = own_ref.shape[0] // 2
    sum_ref[:half] = own_ref[:half] + low_one[:half].astype(F32) + low_two[...].astype(F32)
    sum_ref[half:] = own_ref[half:] + high_two[:half].astype(F32) + high_one[...].astype(F32)
    mine = pl.multiple_of(jnp.bitwise_and(place_ref[1], 1) * half, half)
    keep_ref[...] = sum_ref[pl.ds(mine, half), :]
    send_ref[...] = sum_ref[pl.ds(pl.multiple_of(half - mine, half), half), :].astype(BF16)


def quarter_kernel(place_ref, keep_ref, got_ref, own_ref, send_ref):
    quarter = own_ref.shape[0]
    mine = pl.multiple_of(jnp.right_shift(place_ref[1], 1) * quarter, quarter)
    other = pl.multiple_of(quarter - mine, quarter)
    own_ref[...] = keep_ref[pl.ds(mine, quarter), :] + got_ref[pl.ds(mine, quarter), :].astype(F32)
    send_ref[...] = (
        keep_ref[pl.ds(other, quarter), :] + got_ref[pl.ds(other, quarter), :].astype(F32)
    ).astype(BF16)


def join_kernel(place_ref, own_ref, got_ref, out_ref):
    quarter = own_ref.shape[0]
    mine = pl.multiple_of(jnp.right_shift(place_ref[1], 1) * quarter, quarter)
    out_ref[pl.ds(mine, quarter), :] = own_ref[...]
    out_ref[pl.ds(pl.multiple_of(quarter - mine, quarter), quarter), :] = got_ref[...]


def rows_in_order(place, parts, into):
    quarter = parts[0].shape[0]
    for j, part in enumerate(parts):
        here = pl.ds(pl.multiple_of(jnp.bitwise_xor(place, j) * quarter, quarter), quarter)
        into[here, :] = part[...].astype(F32)


def finish_zo_kernel(place_ref, mine_ref, other_ref, z_ref, o_ref, sum_ref):
    half = mine_ref.shape[0]
    mine = pl.multiple_of(jnp.bitwise_and(place_ref[1], 1) * half, half)
    sum_ref[pl.ds(mine, half), :] = mine_ref[...].astype(F32)
    sum_ref[pl.ds(pl.multiple_of(half - mine, half), half), :] = other_ref[...].astype(F32)
    inner = z_ref.shape[1]
    z_ref[...] = sum_ref[:, :inner]
    o_ref[...] = sum_ref[:, inner:].T


def line_sum_kernel(own_ref, r1, r2, r3, small_ref, out_ref):
    quarter = own_ref.shape[0]
    total = own_ref[...]
    for ref in (r1, r2, r3):
        total = total + ref[...].astype(F32)
    out_ref[:quarter] = total.astype(BF16)
    small = small_ref[...]
    high = small.astype(BF16)
    low = (small - high.astype(F32)).astype(BF16)
    wide = small.shape[1]
    out_ref[quarter:, wide:] = jnp.zeros((16, out_ref.shape[1] - wide), BF16)
    out_ref[quarter:, :wide] = jnp.concatenate([high, low], axis=0)


def finish_x_kernel(place_ref, z_ref, p0, p1, p2, p3, zx_ref, bc_ref, *refs):
    smalls, sum_ref = refs[:-2], refs[-1]
    small_ref = refs[-2]
    quarter = sum_ref.shape[0] // 4
    inner = z_ref.shape[1]
    for j, part in enumerate((p0, p1, p2, p3)):
        here = pl.ds(pl.multiple_of(jnp.bitwise_xor(place_ref[1], j) * quarter, quarter), quarter)
        sum_ref[here, :] = part[:quarter].astype(F32)
    zx_ref[:, 0, :] = z_ref[...]
    zx_ref[:, 1, :] = sum_ref[:, :inner]
    bc_ref[...] = sum_ref[:, inner:].T[:NBC]
    terms = []
    for part in (p0, p1, p2, p3):
        both = part[quarter:].astype(F32)
        terms.append(both[:8] + both[8:])
    total = (terms[0] + terms[1]) + (terms[2] + terms[3])
    small_ref[...] = total[:, : small_ref.shape[1]]
    smalls_out_kernel(small_ref, *smalls)


def hidden_back_kernel(mine_ref, other_ref, hid_ref, inv_ref, gain_ref, cot_ref, out_ref, gn_ref):
    d_normed = mine_ref[...].astype(F32) + other_ref[...].astype(F32)
    hid = hid_ref[...].astype(F32)
    inv = inv_ref[...]
    scaled = hid * inv
    gn_ref[...] = jnp.sum(d_normed * scaled, axis=0, keepdims=True)
    q = d_normed * gain_ref[...]
    mean = jnp.sum(q * scaled, axis=1, keepdims=True) / hid.shape[1]
    out_ref[...] = cot_ref[...].astype(F32) + inv * (q - scaled * mean)


def masks_of(seg_col, seg_row):
    rows = seg_col.shape[0]
    t = lax.broadcasted_iota(jnp.int32, (rows, rows), 0)
    s = lax.broadcasted_iota(jnp.int32, (rows, rows), 1)
    return jnp.where((t >= s) & (seg_col == seg_row), 0.0, -1e30).astype(F32)


def block_kernel(heads, x_ref, b_ref, c_ref, cum_ref, cumr_ref, dtr_ref, marks_ref, segs_ref, y_ref,
                 cb_ref, bias_ref):
    cb_ref[...] = mul(c_ref[...], b_ref[...], NT)
    bias_ref[...] = masks_of(marks_ref[:, 8:9], segs_ref[0:1])
    for h in range(0, heads, 2):
        lanes = slice(h * P_SIZE, h * P_SIZE + PAIR)
        parts = []
        for head in (h, h + 1):
            steps = decay_steps(cum_ref[...], cumr_ref[...], dtr_ref[...], bias_ref[...], head)
            parts.append(mul((steps * cb_ref[...]).astype(BF16), x_ref[:, lanes]))
        y_ref[:, lanes] = two(*parts)


def gate_kernel(pairs, yb_ref, x_ref, c_ref, cum_ref, marks_ref, z_ref, do_ref, skip_ref,
                gain_ref, s1_ref, s2_ref, y_ref, sums_ref):
    cum = cum_ref[...]
    marks = marks_ref[...]
    square = jnp.zeros((cum.shape[0], PAIR), F32)
    cross = square
    for p in range(pairs):
        lanes = slice(p * PAIR, (p + 1) * PAIR)
        entry = marks[:, 6:7] * jnp.exp(pair_of(cum, 2 * p))
        y_ssd = yb_ref[:, lanes] + entry * mul(c_ref[...], s1_ref[:, lanes] + s2_ref[:, lanes])
        y_ref[:, lanes] = y_ssd
        y = y_ssd + skip_ref[:, lanes] * x_ref[:, lanes].astype(F32)
        z = z_ref[:, lanes].astype(F32)
        gated = y * z * jax.nn.sigmoid(z)
        square = square + gated * gated
        cross = cross + gated * (do_ref[:, lanes] * gain_ref[:, lanes])
    lane = lax.broadcasted_iota(jnp.int32, (1, 2), 1)
    sums_ref[...] = jnp.where(
        lane == 0,
        jnp.sum(square, axis=1, keepdims=True),
        jnp.sum(cross, axis=1, keepdims=True),
    )


def norm_kernel(pairs, inner_full, y_ref, x_ref, c_ref, cum_ref, marks_ref, z_ref, do_ref, skip_ref,
                gain_ref, sums_ref, *refs):
    on_ref, dy_ref, dz_ref, gg_ref, back_ref, back16_ref = refs[-6:]
    cum = cum_ref[...]
    marks = marks_ref[...]
    rms = lax.rsqrt(sums_ref[:, 0:1] / inner_full + EPS)
    coef = rms * rms * sums_ref[:, 1:2] / inner_full
    for p in range(pairs):
        lanes = slice(p * PAIR, (p + 1) * PAIR)
        y = y_ref[:, lanes] + skip_ref[:, lanes] * x_ref[:, lanes].astype(F32)
        z = z_ref[:, lanes].astype(F32)
        sig = jax.nn.sigmoid(z)
        silu = z * sig
        normal = y * silu * rms
        d_out = do_ref[:, lanes]
        on_ref[:, lanes] = (normal * gain_ref[:, lanes]).astype(BF16)
        gg_ref[:, lanes] = jnp.sum(d_out * normal, axis=0, keepdims=True)
        d_gated = d_out * gain_ref[:, lanes] * rms - normal * coef
        d_y = (d_gated * silu).astype(BF16)
        dy_ref[:, lanes] = d_y
        dz_ref[:, lanes] = (d_gated * y * sig * (1.0 + z * (1.0 - sig))).astype(BF16)
        entry = marks[:, 6:7] * jnp.exp(pair_of(cum, 2 * p))
        back = mul(c_ref[...], (entry * d_y.astype(F32)).astype(BF16), TN)
        back_ref[:, lanes] = back
        back16_ref[:, lanes] = back.astype(BF16)


def block_back_kernel(heads, dy_ref, x_ref, b_ref, c_ref, cum_ref, cumr_ref, dtr_ref, marks_ref,
                      segs_ref, back_ref, db_ref, dc_ref, cb_ref, bias_ref, dcb_ref):
    cb_ref[...] = mul(c_ref[...], b_ref[...], NT)
    bias_ref[...] = masks_of(marks_ref[:, 8:9], segs_ref[0:1])
    lane = lax.broadcasted_iota(jnp.int32, (1, PAIR), 1)
    for h in range(0, heads, 2):
        lanes = slice(h * P_SIZE, h * P_SIZE + PAIR)
        d_y = dy_ref[:, lanes]
        x = x_ref[:, lanes]
        parts = []
        for head in (h, h + 1):
            steps = decay_steps(cum_ref[...], cumr_ref[...], dtr_ref[...], bias_ref[...], head)
            mix = (steps * cb_ref[...]).astype(BF16)
            own = (lane < P_SIZE) == (head == h)
            both = mul(jnp.where(own, d_y, jnp.zeros_like(d_y)), x, NT) * steps
            if head == 0:
                dcb_ref[...] = both
            else:
                dcb_ref[...] += both
            parts.append(mul(mix, d_y, TN))
        back_ref[:, lanes] = two(*parts)
    d_cb = dcb_ref[...].astype(BF16)
    dc_ref[...] = mul(d_cb, b_ref[...])
    db_ref[...] = mul(d_cb, c_ref[...], TN)


def state_back_kernel(heads, dy_ref, x_ref, b_ref, c_ref, cum_ref, dt_ref, marks_ref,
                      ub_ref, y_ref, db0_ref, dc0_ref, ext_ref, bcext_ref, tx_ref, bx_ref, tbc_ref,
                      bbc_ref, skip_ref, raw_ref, dtb_ref, alog_ref, pick_ref, g1_ref, g2_ref,
                      s1_ref, s2_ref, *refs):
    (shared_ref, rim_ref, rimbc_ref, dpre_ref, small_ref, skipg_ref, in_ref, out_ref, x_sum_ref,
     thr_ref) = refs[-10:]
    cum = cum_ref[...]
    dt = dt_ref[...]
    marks = marks_ref[...]
    rows = cum.shape[0]
    d_b = db0_ref[...]
    d_c = dc0_ref[...]
    for h in range(0, heads, 2):
        lanes = slice(h * P_SIZE, h * P_SIZE + PAIR)
        entry, tail = gains(cum, dt, marks, h)
        d_y16 = dy_ref[:, lanes]
        d_y = d_y16.astype(F32)
        x = x_ref[:, lanes].astype(F32)
        g = g1_ref[:, lanes] + g2_ref[:, lanes]
        s = s1_ref[:, lanes] + s2_ref[:, lanes]
        from_state = tail * mul(b_ref[...], g)
        ub = ub_ref[:, lanes]
        d_xs = skip_ref[:, lanes] * d_y + ub + from_state
        d_b = d_b + mul((tail * x).astype(BF16), g, NT)
        d_c = d_c + mul((entry * d_y).astype(BF16), s, NT)
        head_of = lax.broadcasted_iota(jnp.int32, (PAIR, heads), 0) // P_SIZE + h
        pick = (head_of == lax.broadcasted_iota(jnp.int32, (PAIR, heads), 1)).astype(BF16)

        def per_head(v):
            high = v.astype(BF16)
            low = (v - high.astype(F32)).astype(BF16)
            return mul(high, pick) + mul(low, pick)

        inside = per_head(d_y * y_ref[:, lanes] - x * ub)
        outside = per_head(x * from_state)
        along_x = per_head(x * ub)
        if h == 0:
            in_ref[...] = inside
            out_ref[...] = outside
            x_sum_ref[...] = along_x
        else:
            in_ref[...] += inside
            out_ref[...] += outside
            x_sum_ref[...] += along_x
        skipg_ref[:, lanes] = jnp.sum(d_y * x, axis=0, keepdims=True)
        both = per_head(jnp.sum(g.astype(F32) * s.astype(F32), axis=0, keepdims=True))
        if h == 0:
            thr_ref[...] = both
        else:
            thr_ref[...] += both
        pre = conv_pre(ext_ref[:, lanes].astype(F32), tx_ref[:, lanes], bx_ref[:, lanes], marks)
        sig = jax.nn.sigmoid(pre)
        d_pre = d_xs * sig * (1.0 + pre * (1.0 - sig))
        dpre_ref[:, lanes] = d_pre
        rim_ref[:, lanes] = d_pre[:8]
    last = cum[rows - 1 : rows]
    run_gain = marks[rows - 1 : rows, 6:7] * jnp.exp(last)
    through = run_gain * thr_ref[...]
    d_decay = (
        mul(tri(rows, upper=True), in_ref[...], precision=EXACT)
        + mul(tri(rows, strict=True), out_ref[...], precision=EXACT)
        + through
    )
    dt_in = raw_ref[...] + dtb_ref[...]
    sig = jax.nn.sigmoid(dt_in)
    ratio = jnp.where(dt_in < -20.0, 1.0, sig / jnp.maximum(dt, 1e-30))
    d_raw = (x_sum_ref[...] + out_ref[...]) * ratio - jnp.exp(alog_ref[...]) * d_decay * sig
    high = d_raw.astype(BF16)
    low = (d_raw - high.astype(F32)).astype(BF16)
    shared_ref[:, 2 * N :] = jnp.zeros((rows, TAIL - 2 * N), BF16)
    shared_ref[:, 2 * N : NBC] = (mul(high, pick_ref[...]) + mul(low, pick_ref[...])).astype(BF16)
    small_ref[...] = jnp.zeros(small_ref.shape, F32)
    small_ref[0:1, :heads] = jnp.sum(d_raw, axis=0, keepdims=True)
    small_ref[1:2, :heads] = -jnp.exp(alog_ref[...]) * jnp.sum(dt * d_decay, axis=0, keepdims=True)
    shared_ref[:, :N] = d_b.astype(BF16)
    shared_ref[:, N : 2 * N] = d_c.astype(BF16)
    pre = conv_pre(bcext_ref[...].astype(F32), tbc_ref[...], bbc_ref[...], marks)
    sig = jax.nn.sigmoid(pre)
    slope = sig * (1.0 + pre * (1.0 - sig))
    inner = heads * P_SIZE
    rimbc_ref[:, :N] = d_b[:8].astype(BF16).astype(F32) * slope[:8, :N]
    rimbc_ref[:, N:] = d_c[:8].astype(BF16).astype(F32) * slope[:8, N:]
    rim_ref[:, inner:] = rimbc_ref[...]


def taps_back(d_pre, rim, ext, taps, marks, dv_ref, lanes, grads_ref):
    rows = d_pre.shape[0]
    longer = jnp.concatenate([d_pre, rim], axis=0)
    d_v = taps[KC - 1 : KC] * d_pre
    for shift in range(1, KC):
        moved = pltpu.roll(longer, rows + 8 - shift, 0)[:rows]
        d_v = d_v + taps[KC - 1 - shift : KC - shift] * moved * marks[:, 2 + shift : 3 + shift]
    dv_ref[:, lanes] = d_v.astype(BF16)
    for k in range(KC):
        v = ext[RIM:] if k == KC - 1 else (
            pltpu.roll(ext, KC - 1 - k, 0)[RIM:] * marks[:, k : k + 1]
        )
        grads_ref[k : k + 1, lanes] = jnp.sum(d_pre * v, axis=0, keepdims=True)
    grads_ref[KC : KC + 1, lanes] = jnp.sum(d_pre, axis=0, keepdims=True)


def conv_back_kernel(pairs, dpre_ref, rim_ref, ext_ref, tx_ref, marks_ref, mine_ref, other_ref,
                     rimbc_ref, bcext_ref, tbc_ref, bbc_ref, dx_ref, grads_ref):
    inner = pairs * PAIR
    marks = marks_ref[...]
    for p in range(pairs):
        lanes = slice(p * PAIR, (p + 1) * PAIR)
        taps_back(dpre_ref[:, lanes], rim_ref[:, lanes], ext_ref[:, lanes].astype(F32),
                  tx_ref[:, lanes], marks, dx_ref, lanes, grads_ref)
    ext = bcext_ref[...].astype(F32)
    pre = conv_pre(ext, tbc_ref[...], bbc_ref[...], marks)
    sig = jax.nn.sigmoid(pre)
    shared = mine_ref[...].astype(F32) + other_ref[...].astype(F32)
    d_pre = shared[:, : 2 * N] * sig * (1.0 + pre * (1.0 - sig))
    taps_back(d_pre, rim_ref[:, inner:] + rimbc_ref[...], ext, tbc_ref[...], marks, dx_ref,
              slice(inner, inner + 2 * N), grads_ref)
    dx_ref[:, inner + 2 * N :] = shared[:, 2 * N :].astype(BF16)


def smalls_kernel(seqs, norm_ref, conv_ref, *refs):
    out_ref = refs[-1]
    head, skip, gate = (refs[i * seqs : (i + 1) * seqs] for i in range(3))
    inner = skip[0].shape[1]

    def total(parts):
        return functools.reduce(lambda a, b: a + b, [p[...] for p in parts])

    out_ref[KC + 1 :] = jnp.zeros((8 - KC - 1, out_ref.shape[1]), F32)
    out_ref[: KC + 1] = jnp.sum(conv_ref[:, : KC + 1], axis=0)
    out_ref[5:6, :inner] = jnp.sum(norm_ref[...], axis=0)
    out_ref[6:7, :inner] = total(gate)
    out_ref[7:8, :inner] = total(skip)
    both = total(head)
    out_ref[5:6, inner : inner + PAIR] = both[0:1]
    out_ref[6:7, inner : inner + PAIR] = both[1:2]


def smalls_out_kernel(all_ref, gn_ref, tx_ref, bx_ref, tbc_ref, bbc_ref, dtb_ref, alog_ref, skip_ref,
                      gg_ref):
    inner = gn_ref.shape[1]
    heads = dtb_ref.shape[1]
    tx_ref[...] = all_ref[:KC, :inner]
    tbc_ref[...] = all_ref[:KC, inner:]
    bx_ref[...] = all_ref[KC : KC + 1, :inner]
    bbc_ref[...] = all_ref[KC : KC + 1, inner:]
    gn_ref[...] = all_ref[5:6, :inner]
    gg_ref[...] = all_ref[6:7, :inner]
    dtb_ref[...] = all_ref[5:6, inner : inner + heads]
    alog_ref[...] = all_ref[6:7, inner : inner + heads]
    lane = lax.broadcasted_iota(jnp.int32, (inner, heads), 0) // P_SIZE
    pick = (lane == lax.broadcasted_iota(jnp.int32, (inner, heads), 1)).astype(F32)
    skip_ref[...] = mul(all_ref[7:8, :inner], pick, precision=EXACT)


def launch(order, kernel, name, ins, outs, scratch=(), grid=(1,), into=()):
    def spec(block, index):
        if block is None:
            return pl.BlockSpec(memory_space=pltpu.SMEM)
        return pl.BlockSpec(block, index)

    values = [a for a, _, _ in ins] + list(into)
    if order is not None:
        values = order.after(*values)
    results = pl.pallas_call(
        kernel,
        grid=grid,
        in_specs=[spec(block, index) for _, block, index in ins]
        + [pl.BlockSpec(memory_space=pl.ANY)] * len(into),
        out_specs=[spec(block, index) for _, block, index in outs],
        out_shape=[jax.ShapeDtypeStruct(*form) for form, _, _ in outs],
        scratch_shapes=list(scratch),
        input_output_aliases={len(ins) + i: i for i in range(len(into))},
        compiler_params=pltpu.CompilerParams(vmem_limit_bytes=VMEM),
        cost_estimate=pl.CostEstimate(flops=1, bytes_accessed=1, transcendentals=0),
        name=name,
    )(*values)
    if order is not None:
        order.did(results[0])
    return results


def at(a, b):
    return a, (None,) + a.shape[1:], lambda *_: (b,) + (0,) * (a.ndim - 1)


def own(a):
    return a, (None,) + a.shape[1:], lambda b: (b,) + (0,) * (a.ndim - 1)


def every(a):
    a = a.reshape((1, -1)) if a.ndim == 1 else a
    return a, a.shape, lambda *b: (0,) * a.ndim


def scalar(a):
    return a, None, None


def gives_at(shape, kind, b):
    return (shape, kind), (None,) + shape[1:], lambda *_: (b,) + (0,) * (len(shape) - 1)


def gives_whole(shape, kind):
    return (shape, kind), shape, lambda *b: (0,) * len(shape)


def head_parts(value):
    if lax.axis_size("head") == 2:
        return value, hop(value, "head", 1)
    return lax.psum(value, "head"), jnp.zeros_like(value)


def grads_begin(order, place, lefts, rights):
    wide = sum(r.shape[2] for r in rights)
    quarter = lefts[0].shape[2] // lax.axis_size("fsdp")
    half = quarter // 2
    return launch(
        order,
        functools.partial(weight_grad_kernel, len(lefts), lefts[0].shape[0]),
        "weight_grad",
        [scalar(place)] + [every(a) for a in lefts + rights],
        [
            gives_whole((quarter, wide), F32),
            gives_whole((half, wide), F32),
            gives_whole((half, wide), F32),
            gives_whole((quarter, wide), BF16),
            gives_whole((quarter, wide), BF16),
        ],
    )


def grads_first(terms):
    _, _, _, one, two_way = terms
    return hop(one, "fsdp", 1), hop(two_way, "fsdp", 2)


def grads_second(order, terms, first):
    _, low, high, _, _ = terms
    half = low.shape[0]
    low_one, high_two = order.after(*first)
    low_next = (low + low_one[half:].astype(F32)).astype(BF16)
    high_next = (high + high_two[half:].astype(F32)).astype(BF16)
    order.did(high_next)
    return hop(low_next, "fsdp", 2), hop(high_next, "fsdp", 1)


def grads_quarters(order, place, terms, first, second):
    mine = terms[0]
    quarter = (mine.shape[0] // 4, mine.shape[1])
    return launch(
        order,
        quarters_kernel,
        "quarters",
        [scalar(place)] + [every(a) for a in (mine, first[0], second[0], first[1], second[1])],
        [gives_whole(quarter, F32)] + [gives_whole(quarter, BF16)] * 3,
        [pltpu.VMEM(mine.shape, F32)],
    )


def grads_halves(order, place, terms, first, second):
    mine = terms[0]
    half = (mine.shape[0] // 2, mine.shape[1])
    return launch(
        order,
        halves_kernel,
        "halves",
        [scalar(place)] + [every(a) for a in (mine, first[0], second[0], first[1], second[1])],
        [gives_whole(half, F32), gives_whole(half, BF16)],
        [pltpu.VMEM(mine.shape, F32)],
    )


def line_quarter(order, place, keep, got):
    quarter = (keep.shape[0] // 2, keep.shape[1])
    own_sum, send = launch(
        order,
        quarter_kernel,
        "quarter",
        [scalar(place), every(keep), every(got)],
        [gives_whole(quarter, F32), gives_whole(quarter, BF16)],
    )
    return own_sum, hop(send, "seq", 2)


def line_join(order, place, mine, other):
    (both,) = launch(
        order,
        join_kernel,
        "join",
        [scalar(place), every(mine), every(other)],
        [gives_whole((2 * mine.shape[0], mine.shape[1]), BF16)],
    )
    return both


def small_sum(order, mine, other):
    (other,) = order.after(other)
    return order.did(mine + other)


def line_terms(quarters):
    return [hop(q, "seq", j) for j, q in enumerate(quarters[1:], 1)]


def line_sum(order, mine, terms):
    total = mine
    for term in order.after(*terms):
        total = total + term.astype(F32)
    return order.did(total.astype(BF16))


def line_parts(total):
    return [total] + [hop(total, "seq", j) for j in range(1, 4)]


def shards(
    hidden,
    segment_ids,
    norm_gain,
    w_zx,
    w_bcdt,
    conv_x,
    conv_x_bias,
    conv_bc,
    conv_bc_bias,
    dt_bias,
    a_log,
    d_skip,
    gate_gain,
    w_out,
    cotangent,
):
    head_place = lax.axis_index("head")
    head_count = lax.axis_size("head")
    seq_place = lax.axis_index("seq")
    seq_count = lax.axis_size("seq")
    place = jnp.stack([lax.axis_index("fsdp"), seq_place]).astype(jnp.int32)
    by_blocks = square("fsdp") and square("seq")
    seqs, rows, width = hidden.shape
    own_rows, _, inner = w_zx.shape
    heads = dt_bias.shape[0]
    inner_full = inner * head_count
    longer = rows + RIM
    pairs = heads // 2
    wide_x = inner + TAIL
    each = range(seqs)

    def gives(shape, kind):
        return ((seqs,) + shape, kind), (None,) + shape, lambda b: (b,) + (0,) * len(shape)

    order = Order()

    if by_blocks:
        half = own_rows // 2
        x_low, x_high = launch(
            order,
            pack_x_kernel,
            "pack_x",
            [every(w_zx), every(w_bcdt.T)],
            [gives_whole((half, wide_x), BF16)] * 2,
        )
        w_x = gather_halves(order, x_low, x_high, "fsdp")
    else:
        x_own = jnp.concatenate([w_zx[:, 1], jnp.pad(w_bcdt, ((0, 0), (0, TAIL - NBC)))], axis=1)
        w_x = lax.all_gather(x_own, "fsdp", axis=0, tiled=True)
        zo_own = jnp.concatenate([w_zx[:, 0], w_out.T], axis=1)
        w_zo = lax.all_gather(zo_own, "fsdp", axis=0, tiled=True)

    def input_norm(part):
        part = part.astype(F32)
        inv = lax.rsqrt(jnp.mean(part * part, axis=-1, keepdims=True) + EPS)
        return (part * inv * norm_gain).astype(BF16), inv

    before = step_along(hidden[:, rows - RIM :], "seq", 1)
    normed, inv_rms = input_norm(hidden)

    edge = KC - 1
    seg_ids, before = order.after(segment_ids, before)
    seg_padded = jnp.pad(seg_ids, ((0, 0), (edge, 0)), constant_values=-1)
    seg_padded = jnp.pad(seg_padded, ((0, 0), (0, edge)), constant_values=-2)
    seg_wide = lax.dynamic_slice_in_dim(seg_padded, seq_place * rows, rows + 2 * edge, 1).astype(F32)
    seg = seg_wide[:, edge : edge + rows]
    near = [seg] + [seg_wide[:, k : k + rows] for k in range(edge)]
    near += [seg_wide[:, edge + k : edge + k + rows] for k in range(1, KC)]
    near += [jnp.broadcast_to(s, seg.shape) for s in (seg_wide[:, edge - 1 : edge], seg[:, -1:])]
    segs = jnp.pad(jnp.stack(near, axis=1), ((0, 0), (0, 16 - len(near)), (0, 0)))
    head_pick = (
        jnp.arange(heads)[:, None] + head_place * heads == jnp.arange(NH)[None, :]
    ).astype(BF16)
    normed_rim, _ = input_norm(before)
    order.did(segs)
    (normed_rim,) = order.after(normed_rim)
    order.did(normed_rim)

    if by_blocks:
        (zo_own,) = launch(
            order,
            pack_zo_kernel,
            "pack_zo",
            [every(w_zx), every(w_out)],
            [gives_whole((own_rows, 2 * inner), BF16)],
        )
        zo_own, w_x[6], w_x[7] = lax.optimization_barrier((zo_own, w_x[6], w_x[7]))
        zo_gathered = gather_first(zo_own, "fsdp")

    def project(b, into):
        if by_blocks:
            return launch(
                order,
                input_kernel,
                "input",
                [scalar(place), at(normed_rim, b), at(normed, b)] + [every(w) for w in w_x],
                [
                    gives_at((seqs, longer, inner), BF16, b),
                    gives_at((seqs, longer, 2 * N), BF16, b),
                    gives_at((seqs, rows, NH), BF16, b),
                ],
                into=into,
            )
        proj = jnp.dot(
            jnp.concatenate([normed_rim, normed], axis=1), w_x, preferred_element_type=F32
        ).astype(BF16)
        return (
            proj[..., :inner],
            proj[..., inner : inner + 2 * N],
            proj[:, RIM:, inner + 2 * N : inner + NBC],
        )

    conv_params = [every(conv_x), every(conv_x_bias), every(conv_bc), every(conv_bc_bias)]

    def convolve(b, x_ext, bc_ext, dt_all, into):
        return launch(
            order,
            functools.partial(conv_kernel, pairs),
            "conv",
            [at(x_ext, b), at(bc_ext, b), at(dt_all, b), every(head_pick), at(segs, b)]
            + conv_params
            + [every(dt_bias), every(a_log), every(d_skip)],
            [
                gives_at((seqs,) + shape, kind, b)
                for shape, kind in (
                    ((rows, inner), BF16),
                    ((rows, N), BF16),
                    ((rows, N), BF16),
                    ((rows, heads), F32),
                    ((rows, heads), F32),
                    ((heads, rows), F32),
                    ((heads, rows), F32),
                    ((rows, heads), F32),
                    ((rows, 16), F32),
                )
            ]
            + [
                gives_whole((1, inner), F32),
                gives_whole((N, inner), F32),
                gives_whole((N, inner), BF16),
                gives_whole((1, inner), F32),
            ],
            into=into,
        )

    def onward(lap, entered, moving, own_state, gain, steps):
        (moving,) = order.after(moving)
        entered = moving if entered is None else entered + moving
        leaving = order.did((gain * entered.astype(F32) + own_state).astype(BF16))
        return entered, pass_along(leaving, "seq", lap, steps)

    def nothing(state):
        return jnp.zeros(state.shape, BF16)

    def depart(sent, steps):
        if seq_count == 1:
            return None, nothing(sent)
        return None, pass_along(sent, "seq", 0, steps)

    def arrive(chain):
        entered, moving = chain
        return [nothing(moving) if entered is None else entered, moving]

    ext = ()
    parts = []
    moving = []
    for b in each:
        ext = project(b, ext)
        parts.append(convolve(b, *ext, parts[-1][:9] if parts else ()))
        moving.append(depart(parts[b][11], 1))
    xs, bs, cs, cum, dt, cum_rows, dt_rows, raw, marks = parts[-1][:9]
    run_gain, fresh, _, skips = zip(*[p[9:] for p in parts])
    skip = skips[0]

    square_form = pltpu.VMEM((rows, rows), F32)

    laps = range(1, seq_count - 1)
    for lap in laps[:1]:
        moving = [onward(lap, *moving[b], fresh[b], run_gain[b], 1) for b in each]
    if by_blocks:
        w_zo = gather_second(order, zo_own, zo_gathered, "fsdp")
    (y_block,) = launch(
        order,
        functools.partial(block_kernel, heads),
        "block",
        [own(a) for a in (xs, bs, cs, cum, cum_rows, dt_rows, marks, segs)],
        [gives((rows, inner), F32)],
        [square_form] * 2,
        grid=(seqs,),
    )
    for lap in laps[1:]:
        moving = [onward(lap, *moving[b], fresh[b], run_gain[b], 1) for b in each]
    state_in = [arrive(m) for m in moving]

    if by_blocks:
        z, d_outn = launch(
            order,
            gate_in_kernel,
            "gate_in",
            [scalar(place), own(normed), own(cotangent)] + [every(w) for w in w_zo],
            [gives((rows, inner), BF16), gives((rows, inner), F32)],
            grid=(seqs,),
        )
    else:
        z = jnp.dot(normed, w_zo[:, :inner], preferred_element_type=F32).astype(BF16)
        d_outn = jnp.dot(cotangent, w_zo[:, inner:], preferred_element_type=F32)

    def gate(b):
        y_ssd, sums = launch(
            order,
            functools.partial(gate_kernel, pairs),
            "gate",
            [at(a, b) for a in (y_block, xs, cs, cum, marks, z, d_outn)]
            + [every(skip), every(gate_gain), every(state_in[b][0]), every(state_in[b][1])],
            [gives_whole((rows, inner), F32), gives_whole((rows, 2), F32)],
        )
        return y_ssd, sum_all(sums, ("head",))

    def norm(b, y_ssd, sums, into):
        return launch(
            order,
            functools.partial(norm_kernel, pairs, inner_full),
            "norm",
            [every(y_ssd)]
            + [at(a, b) for a in (xs, cs, cum, marks, z, d_outn)]
            + [every(skip), every(gate_gain), every(sums)],
            [gives_at((seqs, rows, inner), BF16, b)] * 3
            + [
                gives_whole((1, inner), F32),
                gives_whole((N, inner), F32),
                gives_whole((N, inner), BF16),
            ],
            into=into,
        )

    y_ssd = []
    normals = []
    moving = []
    for b in each:
        y_b, sums = gate(b)
        y_ssd.append(y_b)
        normals.append(norm(b, y_b, sums, normals[-1][:3] if normals else ()))
        moving.append(depart(normals[b][5], -1))
    out_norm, d_y, d_z = normals[-1][:3]
    grad_gate, back, _ = zip(*[n[3:] for n in normals])

    x_ext, bc_ext, _ = ext


    def back_lap(lap):
        return [onward(lap, *moving[b], back[b], run_gain[b], -1) for b in each]

    if by_blocks:
        zo_terms = grads_begin(order, place, [normed, cotangent], [d_z, out_norm])
        zo_first = grads_first(zo_terms)
    for lap in laps[:1]:
        moving = back_lap(lap)
    back_x, d_b, d_c = launch(
        order,
        functools.partial(block_back_kernel, heads),
        "block_back",
        [own(a) for a in (d_y, xs, bs, cs, cum, cum_rows, dt_rows, marks, segs)],
        [gives((rows, inner), F32), gives((rows, N), F32), gives((rows, N), F32)],
        [square_form] * 3,
        grid=(seqs,),
    )
    for lap in laps[1:]:
        moving = back_lap(lap)
    if by_blocks:
        mixed, by_z = launch(
            order,
            output_kernel,
            "output",
            [scalar(place), own(out_norm), own(d_z)] + [every(w) for w in w_zo],
            [gives((rows, width), kind) for kind in (BF16, F32)],
            grid=(seqs,),
        )
    else:
        last = (((2,), (1,)), ((), ()))
        mixed = mul(out_norm, w_zo[:, inner:], last).astype(BF16)
        by_z = mul(d_z, w_zo[:, :inner], last)
    mixed, mixed_other = head_parts(mixed)
    grad_state = [arrive(m) for m in moving]

    def state_back(b, into):
        return launch(
            order,
            functools.partial(state_back_kernel, heads),
            "state_back",
            [at(a, b) for a in (d_y, xs, bs, cs, cum, dt, marks)]
            + [at(back_x, b), every(y_ssd[b]), at(d_b, b), at(d_c, b), at(x_ext, b), at(bc_ext, b)]
            + conv_params
            + [every(skip), at(raw, b)]
            + [every(a) for a in (dt_bias, a_log, head_pick, *grad_state[b], *state_in[b])],
            [
                gives_at((seqs, rows, TAIL), BF16, b),
                gives_at((seqs, 8, inner + 2 * N), F32, b),
                gives_at((seqs, 8, 2 * N), F32, b),
                gives_at((seqs, rows, inner), F32, b),
                gives_whole((2, PAIR), F32),
                gives_whole((1, inner), F32),
            ],
            [pltpu.VMEM((rows, heads), F32)] * 3 + [pltpu.VMEM((1, heads), F32)],
            into=into,
        )

    def neighbours(shared, rim, rim_bc):
        rim_other = jnp.zeros_like(rim_bc)
        for turn in range(1, head_count):
            rim_other = rim_other + lax.ppermute(
                rim_bc,
                ("seq", "head"),
                [
                    (s * head_count + p, (s - 1) * head_count + (p + turn) % head_count)
                    for s in range(1, seq_count)
                    for p in range(head_count)
                ],
            )
        return head_parts(shared) + (step_along(rim, "seq", -1), rim_other)

    state_parts = []
    together = ()
    for b in each:
        state_parts.append(state_back(b, together))
        together = state_parts[b][:4]
        if by_blocks and b == 0:
            zo_second = grads_second(order, zo_terms, zo_first)
    near_parts = neighbours(*together[:3])
    (block_out,) = launch(
        order,
        block_out_kernel,
        "block_out",
        [every(hidden), every(mixed), every(mixed_other)],
        [gives_whole((seqs, rows, width), BF16)],
    )
    if by_blocks:
        zo_keep, zo_send = grads_halves(order, place, zo_terms, zo_first, zo_second)
        zo_half = hop(zo_send, "seq", 1)
    shared, shared_other, rim, rim_other = near_parts
    d_xb, grad_conv = launch(
        order,
        functools.partial(conv_back_kernel, pairs),
        "conv_back",
        [own(together[3]), own(rim), own(x_ext), every(conv_x), own(marks)]
        + [own(a) for a in (shared, shared_other, rim_other, bc_ext)]
        + [every(conv_bc), every(conv_bc_bias)],
        [gives((rows, wide_x), BF16), gives((8, inner + 2 * N), F32)],
        grid=(seqs,),
    )
    small = [s[4] for s in state_parts]
    grad_skip = [s[5] for s in state_parts]

    if by_blocks:
        x_terms = grads_begin(order, place, [normed], [d_xb])
        x_first = grads_first(x_terms)
        (by_head,) = launch(
            order,
            functools.partial(input_back_kernel, head_count),
            "input_back",
            [scalar(place), own(d_xb), own(by_z)] + [every(w) for w in w_x],
            [gives((rows, width), BF16)],
            grid=(seqs,),
        )
    else:
        dxb = d_xb
        by_head = (
            by_z
            + mul(dxb[..., :inner], w_x[:, :inner], last)
            + mul(dxb[..., inner:], w_x[:, inner:], last) / head_count
        ).astype(BF16)
    by_head, by_other = head_parts(by_head)
    if by_blocks:
        zo_own, zo_quarter = line_quarter(order, place, zo_keep, zo_half)
        x_second = grads_second(order, x_terms, x_first)
    grad_hidden, grad_norm = launch(
        order,
        hidden_back_kernel,
        "hidden_back",
        [own(by_head), own(by_other), own(hidden), own(inv_rms), every(norm_gain), own(cotangent)],
        [gives((rows, width), F32), gives((1, width), F32)],
        grid=(seqs,),
    )

    (flat,) = launch(
        order,
        functools.partial(smalls_kernel, seqs),
        "smalls",
        [every(grad_norm), every(grad_conv)]
        + [every(a) for part in (small, grad_skip, grad_gate) for a in part],
        [gives_whole((8, inner + 2 * N), F32)],
    )

    small_forms = [
        gives_whole(shape, F32)
        for shape in (
            (1, width),
            (KC, inner),
            (1, inner),
            (KC, 2 * N),
            (1, 2 * N),
            (1, heads),
            (1, heads),
            (1, heads),
            (1, inner),
        )
    ]

    if by_blocks:
        small_hop = hop(flat, "fsdp", 1)
        zo_own = line_sum(order, zo_own, [zo_quarter])
        zo_quarter = hop(zo_own, "seq", 2)
        x_quarters = grads_quarters(order, place, x_terms, x_first, x_second)
        x_line = line_terms(x_quarters)
        (x_line[0],) = order.after(x_line[0])
        order.did(x_line[0])
        zo_mine = line_join(order, place, zo_own, zo_quarter)
        zo_other = hop(zo_mine, "seq", 1)
        flat = small_sum(order, flat, small_hop)
        flat = small_sum(order, flat, hop(flat, "fsdp", 2))
        (x_total,) = launch(
            order,
            line_sum_kernel,
            "line_sum",
            [every(a) for a in (x_quarters[0], *x_line, flat)],
            [gives_whole((own_rows // 4 + 16, wide_x), BF16)],
        )
        x_parts = line_parts(x_total)
        grad_z, grad_o = launch(
            order,
            finish_zo_kernel,
            "finish_zo",
            [scalar(place), every(zo_mine), every(zo_other)],
            [gives_whole((own_rows, inner), F32), gives_whole((inner, own_rows), F32)],
            [pltpu.VMEM((own_rows, 2 * inner), F32)],
        )
        grad_zx, grad_bcdt, *summed = launch(
            order,
            finish_x_kernel,
            "finish_x",
            [scalar(place), every(grad_z)] + [every(a) for a in x_parts],
            [gives_whole((own_rows, 2, inner), F32), gives_whole((NBC, own_rows), F32)]
            + small_forms,
            [pltpu.VMEM((8, inner + 2 * N), F32), pltpu.VMEM((own_rows, wide_x), F32)],
        )
        grad_bcdt = grad_bcdt.T
    else:
        flat = sum_all(flat, ("seq", "fsdp"))
        summed = launch(order, smalls_out_kernel, "smalls_out", [every(flat)], small_forms)
        def owned(left, right):
            full = lax.dot_general(
                left, right, (((0, 1), (0, 1)), ((), ())), preferred_element_type=F32
            )
            return lax.psum(lax.psum_scatter(full, "fsdp", scatter_dimension=0, tiled=True), "seq")

        grad_x = owned(normed, d_xb)
        grad_zx = jnp.stack([owned(normed, d_z), grad_x[:, :inner]], axis=1)
        grad_bcdt = grad_x[:, inner : inner + NBC]
        grad_o = owned(cotangent, out_norm).T
    grad_norm, grad_tx, grad_bx, grad_tbc, grad_bbc, grad_dtb, grad_alog, grad_skip, grad_gate = summed
    return (
        block_out,
        grad_hidden,
        grad_norm.reshape(-1),
        grad_zx,
        grad_bcdt,
        grad_tx,
        grad_bx.reshape(-1),
        grad_tbc,
        grad_bbc.reshape(-1),
        grad_dtb.reshape(-1),
        grad_alog.reshape(-1),
        grad_skip.reshape(-1),
        grad_gate.reshape(-1),
        grad_o,
    )


def solution(mesh):
    placed = (
        P("fsdp", "seq", None),
        P("fsdp", None),
        P(),
        P("fsdp", None, "head"),
        P("fsdp", None),
        P(None, "head"),
        P("head"),
        P(),
        P(),
        P("head"),
        P("head"),
        P("head"),
        P("head"),
        P("head", "fsdp"),
        P("fsdp", "seq", None),
    )
    return jax.shard_map(
        shards,
        mesh=mesh,
        in_specs=placed,
        out_specs=(
            P("fsdp", "seq", None),
            P("fsdp", "seq", None),
            P(),
            P("fsdp", None, "head"),
            P("fsdp", None),
            P(None, "head"),
            P("head"),
            P(),
            P(),
            P("head"),
            P("head"),
            P("head"),
            P("head"),
            P("head", "fsdp"),
        ),
        check_vma=False,
    )
```

```python
import functools

import jax
import jax.numpy as jnp
from jax import lax
from jax.experimental import pallas as pl
from jax.experimental.pallas import tpu as pltpu
from jax.sharding import PartitionSpec as P

P_SIZE = 64
N = 128
NH = 32
KC = 4
NBC = 288
TAIL = 384
RIM = 16
PAIR = 128

EPS = 1e-05
F32 = jnp.float32
BF16 = jnp.bfloat16
EXACT = lax.Precision.HIGHEST
VMEM = 24 * 2**20


def hop(value, axis, bit):
    return lax.ppermute(value, axis, [(i, i ^ bit) for i in range(lax.axis_size(axis))])


def step_along(value, axis, steps):
    count = lax.axis_size(axis)
    initial, last = (max(0, -steps), min(count, count - steps))
    return lax.ppermute(value, axis, [(source, source + steps) for source in range(initial, last)])


class Order:
    def __init__(self):
        self.last = None

    def after(self, *values):
        if self.last is None:
            return values
        return lax.optimization_barrier(values + (self.last,))[:-1]

    def did(self, value):
        self.last = value
        return value


def pass_along(value, axis, lap, steps):
    source = lap if steps > 0 else lax.axis_size(axis) - 1 - lap
    return lax.ppermute(value, axis, [(source, source + steps)])


def square(axis):
    return lax.axis_size(axis) == 4


def tie(value, *others):
    return lax.optimization_barrier((value,) + others)[0]


def gather_halves(order, low, high, axis):
    low_one = hop(low, axis, 1)
    high_two = hop(high, axis, 2)
    high_one = hop(high, axis, 1)
    low_two = hop(low, axis, 2)
    low_one, high_two, high_one, low_two = order.after(low_one, high_two, high_one, low_two)
    order.did(low_one)
    low_three = hop(low_one, axis, 2)
    high_three = hop(high_two, axis, 1)
    return [low, high, low_one, high_one, low_two, high_two, low_three, high_three]


def gather_first(both, axis):
    return hop(both, axis, 1), hop(both, axis, 2)


def gather_second(order, both, first, axis):
    half = both.shape[0] // 2
    one, two = order.after(*first)
    order.did(one)
    low_three = hop(one[:half], axis, 2)
    high_three = hop(two[half:], axis, 1)
    return [both, one, two, low_three, high_three]


def sum_all(value, axes):
    for axis in axes:
        count = lax.axis_size(axis)
        if count & (count - 1):
            value = lax.psum(value, axis)
            continue
        bit = 1
        while bit < count:
            value = value + hop(value, axis, bit)
            bit *= 2
    return value


NT = (((1,), (1,)), ((), ()))
TN = (((0,), (0,)), ((), ()))
NN = (((1,), (0,)), ((), ()))


def mul(a, b, dims=NN, precision=None):
    return lax.dot_general(a, b, dims, precision=precision, preferred_element_type=F32)


def tri(rows, strict=False, upper=False):
    t = lax.broadcasted_iota(jnp.int32, (rows, rows), 0)
    s = lax.broadcasted_iota(jnp.int32, (rows, rows), 1)
    if upper:
        t, s = s, t
    return jnp.where(t > s if strict else t >= s, 1.0, 0.0).astype(F32)


def two(left, right):
    lane = lax.broadcasted_iota(jnp.int32, (1, PAIR), 1)
    return jnp.where(lane < P_SIZE, left, right)


def pair_of(columns, head):
    return two(columns[:, head : head + 1], columns[:, head + 1 : head + 2])


def conv_pre(ext, taps, bias, marks):
    pre = bias + taps[KC - 1 : KC] * ext[RIM:]
    for k in range(KC - 1):
        pre = pre + taps[k : k + 1] * pltpu.roll(ext, KC - 1 - k, 0)[RIM:] * marks[:, k : k + 1]
    return pre


def gains(cum, dt, marks, head):
    rows = cum.shape[0]
    cum_pair = pair_of(cum, head)
    last = two(cum[rows - 1 : rows, head : head + 1], cum[rows - 1 : rows, head + 1 : head + 2])
    entry = marks[:, 6:7] * jnp.exp(cum_pair)
    tail = marks[:, 7:8] * jnp.exp(last - cum_pair) * pair_of(dt, head)
    return entry, tail


def decay_steps(cum, cum_rows, dt_rows, bias, head):
    return (
        jnp.exp(cum[:, head : head + 1] - cum_rows[head : head + 1] + bias)
        * dt_rows[head : head + 1]
    )


def block_lanes(ref, place, j):
    width = ref.shape[1] // 4
    return ref[:, pl.ds(pl.multiple_of(jnp.bitwise_xor(place, j) * width, width), width)]


def both_halves(refs, j, lanes=slice(None)):
    if len(refs) == 5 and j < 3:
        return refs[j][:, lanes]
    if len(refs) == 5:
        return jnp.concatenate([refs[3][:, lanes], refs[4][:, lanes]], axis=0)
    return jnp.concatenate([refs[2 * j][:, lanes], refs[2 * j + 1][:, lanes]], axis=0)


def pack_x_kernel(w_ref, bc_ref, low_ref, high_ref):
    half = w_ref.shape[0] // 2
    inner = w_ref.shape[2]
    low_ref[:, :inner] = w_ref[:half, 1, :]
    high_ref[:, :inner] = w_ref[half:, 1, :]
    turned = bc_ref[...].astype(F32).T.astype(BF16)
    for ref, part in ((low_ref, turned[:half]), (high_ref, turned[half:])):
        ref[:, inner + 2 * N :] = jnp.zeros((half, TAIL - 2 * N), BF16)
        ref[:, inner : inner + NBC] = part


def pack_zo_kernel(w_ref, o_ref, out_ref):
    inner = w_ref.shape[2]
    out_ref[:, :inner] = w_ref[:, 0, :]
    out_ref[:, inner:] = o_ref[...].astype(F32).T.astype(BF16)


def input_kernel(place_ref, rim_ref, n_ref, *refs):
    x_ref, bc_ref, dt_ref = refs[-3:]
    weights = refs[:8]
    inner = x_ref.shape[1]
    place = place_ref[0]
    proj = 0.0
    for j in range(4):
        rows = jnp.concatenate([block_lanes(rim_ref, place, j), block_lanes(n_ref, place, j)], axis=0)
        proj = proj + mul(rows, both_halves(weights, j))
    x_ref[...] = proj[:, :inner].astype(BF16)
    bc_ref[...] = proj[:, inner : inner + 2 * N].astype(BF16)
    dt_ref[...] = proj[RIM:, inner + 2 * N : inner + NBC].astype(BF16)


def conv_kernel(pairs, x_ref, bc_ref, dtall_ref, pick_ref, segs_ref, tx_ref, bx_ref, tbc_ref, bbc_ref,
                dtb_ref, alog_ref, dskip_ref, *refs):
    (xs_ref, b_ref, c_ref, cum_ref, dto_ref, cumr_ref, dtr_ref, raw_ref, marks_ref, run_ref,
     fresh_ref, fresh16_ref, skip_ref) = refs[-13:]
    segs = segs_ref[...]
    rows = segs.shape[1]
    same = jnp.where(segs[1:9] == segs[0:1], 1.0, 0.0)
    marks = jnp.concatenate([same, segs[0:8], jnp.zeros((PAIR - 16, rows), F32)], axis=0).T
    marks_ref[...] = marks[:, :16]
    heads = pick_ref.shape[0]
    spread = (
        lax.broadcasted_iota(jnp.int32, (heads, pairs * PAIR), 1) // P_SIZE
        == lax.broadcasted_iota(jnp.int32, (heads, pairs * PAIR), 0)
    ).astype(F32)
    skip_ref[...] = mul(dskip_ref[...], spread, precision=EXACT)
    pre = conv_pre(bc_ref[...].astype(F32), tbc_ref[...], bbc_ref[...], marks)
    act = (pre * jax.nn.sigmoid(pre)).astype(BF16)
    b_rows = act[:, :N]
    b_ref[...] = b_rows
    c_ref[...] = act[:, N:]
    dt_raw = mul(dtall_ref[...], pick_ref[...], NT)
    raw_ref[...] = dt_raw
    raw = dt_raw + dtb_ref[...]
    dt = jnp.maximum(raw, 0.0) + jnp.log1p(jnp.exp(-jnp.abs(raw)))
    cum = mul(tri(rows), dt * -jnp.exp(alog_ref[...]), precision=EXACT)
    cum_ref[...] = cum
    dto_ref[...] = dt
    wide = jnp.concatenate([cum, dt, jnp.zeros((rows, PAIR - 2 * heads), F32)], axis=1)
    turned = wide.T
    cumr_ref[...] = turned[:heads]
    dtr_ref[...] = turned[heads : 2 * heads]
    for p in range(pairs):
        lanes = slice(p * PAIR, (p + 1) * PAIR)
        pre = conv_pre(x_ref[:, lanes].astype(F32), tx_ref[:, lanes], bx_ref[:, lanes], marks)
        act = (pre * jax.nn.sigmoid(pre)).astype(BF16)
        xs_ref[:, lanes] = act
        entry, tail = gains(cum, dt, marks, 2 * p)
        run_ref[:, lanes] = entry[rows - 1 :]
        fresh = mul(b_rows, (tail * act.astype(F32)).astype(BF16), TN)
        fresh_ref[:, lanes] = fresh
        fresh16_ref[:, lanes] = fresh.astype(BF16)


def gate_in_kernel(place_ref, n_ref, cot_ref, *refs):
    z_ref, do_ref = refs[-2:]
    weights = refs[:-2]
    inner = z_ref.shape[1]
    place = place_ref[0]
    z = 0.0
    d_out = 0.0
    for j in range(4):
        z = z + mul(block_lanes(n_ref, place, j), both_halves(weights, j, slice(0, inner)))
        d_out = d_out + mul(
            block_lanes(cot_ref, place, j), both_halves(weights, j, slice(inner, 2 * inner))
        )
    z_ref[...] = z.astype(BF16)
    do_ref[...] = d_out


def output_kernel(place_ref, on_ref, dz_ref, *refs):
    weights = refs[:-2]
    mixed_ref, byz_ref = refs[-2:]
    inner = on_ref.shape[1]
    quarter = mixed_ref.shape[1] // 4
    place = place_ref[0]
    for j in range(4):
        here = pl.ds(pl.multiple_of(jnp.bitwise_xor(place, j) * quarter, quarter), quarter)
        w = both_halves(weights, j)
        byz_ref[:, here] = mul(dz_ref[...], w[:, :inner], NT)
        mixed_ref[:, here] = mul(on_ref[...], w[:, inner:], NT).astype(BF16)


def block_out_kernel(hid_ref, mine_ref, other_ref, out_ref):
    mixed = mine_ref[...].astype(F32) + other_ref[...].astype(F32)
    out_ref[...] = (hid_ref[...].astype(F32) + mixed).astype(BF16)


def input_back_kernel(head_count, place_ref, dxb_ref, byz_ref, *refs):
    weights, out_ref = refs[:-1], refs[-1]
    inner = dxb_ref.shape[1] - TAIL
    quarter = out_ref.shape[1] // 4
    place = place_ref[0]
    for j in range(4):
        here = pl.ds(pl.multiple_of(jnp.bitwise_xor(place, j) * quarter, quarter), quarter)
        w = both_halves(weights, j)
        out_ref[:, here] = (
            byz_ref[:, here]
            + mul(dxb_ref[:, :inner], w[:, :inner], NT)
            + mul(dxb_ref[:, inner:], w[:, inner:], NT) / head_count
        ).astype(BF16)


def weight_grad_kernel(count, seqs, place_ref, *refs):
    lefts, rights = refs[:count], refs[count : 2 * count]
    own_ref, low_ref, high_ref, one_ref, two_ref = refs[2 * count :]
    half = own_ref.shape[0] // 2
    quarter = own_ref.shape[0]
    place = place_ref[0]
    start = 0
    for i, left in enumerate(lefts):
        wide = rights[i].shape[2]
        cols = slice(start, start + wide)
        start += wide
        for j in (1, 3, 2, 0):
            here = pl.ds(pl.multiple_of(jnp.bitwise_xor(place, j) * quarter, quarter), quarter)
            g = 0.0
            for b in range(seqs):
                g = g + mul(left[b, :, here], rights[i][b], TN)
            low, high = g[:half], g[half:]
            if j == 0:
                own_ref[:, cols] = g
            elif j == 1:
                one_ref[:half, cols] = low.astype(BF16)
                high_ref[:, cols] = high
            elif j == 2:
                two_ref[:half, cols] = high.astype(BF16)
                low_ref[:, cols] = low
            else:
                one_ref[half:, cols] = low.astype(BF16)
                two_ref[half:, cols] = high.astype(BF16)


def quarters_kernel(place_ref, own_ref, low_one, low_two, high_two, high_one, own_q, q1, q2, q3, sum_ref):
    half = own_ref.shape[0] // 2
    quarter = own_ref.shape[0] // 4
    sum_ref[:half] = own_ref[:half] + low_one[:half].astype(F32) + low_two[...].astype(F32)
    sum_ref[half:] = own_ref[half:] + high_two[:half].astype(F32) + high_one[...].astype(F32)
    place = place_ref[1]
    for j, ref in enumerate((own_q, q1, q2, q3)):
        here = pl.ds(pl.multiple_of(jnp.bitwise_xor(place, j) * quarter, quarter), quarter)
        ref[...] = sum_ref[here, :].astype(ref.dtype)


def halves_kernel(place_ref, own_ref, low_one, low_two, high_two, high_one, keep_ref, send_ref, sum_ref):
    half = own_ref.shape[0] // 2
    sum_ref[:half] = own_ref[:half] + low_one[:half].astype(F32) + low_two[...].astype(F32)
    sum_ref[half:] = own_ref[half:] + high_two[:half].astype(F32) + high_one[...].astype(F32)
    mine = pl.multiple_of(jnp.bitwise_and(place_ref[1], 1) * half, half)
    keep_ref[...] = sum_ref[pl.ds(mine, half), :]
    send_ref[...] = sum_ref[pl.ds(pl.multiple_of(half - mine, half), half), :].astype(BF16)


def quarter_kernel(place_ref, keep_ref, got_ref, own_ref, send_ref):
    quarter = own_ref.shape[0]
    mine = pl.multiple_of(jnp.right_shift(place_ref[1], 1) * quarter, quarter)
    other = pl.multiple_of(quarter - mine, quarter)
    own_ref[...] = keep_ref[pl.ds(mine, quarter), :] + got_ref[pl.ds(mine, quarter), :].astype(F32)
    send_ref[...] = (
        keep_ref[pl.ds(other, quarter), :] + got_ref[pl.ds(other, quarter), :].astype(F32)
    ).astype(BF16)


def join_kernel(place_ref, own_ref, got_ref, out_ref):
    quarter = own_ref.shape[0]
    mine = pl.multiple_of(jnp.right_shift(place_ref[1], 1) * quarter, quarter)
    out_ref[pl.ds(mine, quarter), :] = own_ref[...]
    out_ref[pl.ds(pl.multiple_of(quarter - mine, quarter), quarter), :] = got_ref[...]


def rows_in_order(place, parts, into):
    quarter = parts[0].shape[0]
    for j, part in enumerate(parts):
        here = pl.ds(pl.multiple_of(jnp.bitwise_xor(place, j) * quarter, quarter), quarter)
        into[here, :] = part[...].astype(F32)


def finish_zo_kernel(place_ref, mine_ref, other_ref, z_ref, o_ref, sum_ref):
    half = mine_ref.shape[0]
    mine = pl.multiple_of(jnp.bitwise_and(place_ref[1], 1) * half, half)
    sum_ref[pl.ds(mine, half), :] = mine_ref[...].astype(F32)
    sum_ref[pl.ds(pl.multiple_of(half - mine, half), half), :] = other_ref[...].astype(F32)
    inner = z_ref.shape[1]
    z_ref[...] = sum_ref[:, :inner]
    o_ref[...] = sum_ref[:, inner:].T


def line_sum_kernel(own_ref, r1, r2, r3, small_ref, out_ref):
    quarter = own_ref.shape[0]
    total = own_ref[...]
    for ref in (r1, r2, r3):
        total = total + ref[...].astype(F32)
    out_ref[:quarter] = total.astype(BF16)
    small = small_ref[...]
    high = small.astype(BF16)
    low = (small - high.astype(F32)).astype(BF16)
    wide = small.shape[1]
    out_ref[quarter:, wide:] = jnp.zeros((16, out_ref.shape[1] - wide), BF16)
    out_ref[quarter:, :wide] = jnp.concatenate([high, low], axis=0)


def finish_x_kernel(place_ref, z_ref, p0, p1, p2, p3, zx_ref, bc_ref, *refs):
    smalls, sum_ref = refs[:-2], refs[-1]
    small_ref = refs[-2]
    quarter = sum_ref.shape[0] // 4
    inner = z_ref.shape[1]
    for j, part in enumerate((p0, p1, p2, p3)):
        here = pl.ds(pl.multiple_of(jnp.bitwise_xor(place_ref[1], j) * quarter, quarter), quarter)
        sum_ref[here, :] = part[:quarter].astype(F32)
    zx_ref[:, 0, :] = z_ref[...]
    zx_ref[:, 1, :] = sum_ref[:, :inner]
    bc_ref[...] = sum_ref[:, inner:].T[:NBC]
    terms = []
    for part in (p0, p1, p2, p3):
        both = part[quarter:].astype(F32)
        terms.append(both[:8] + both[8:])
    total = (terms[0] + terms[1]) + (terms[2] + terms[3])
    small_ref[...] = total[:, : small_ref.shape[1]]
    smalls_out_kernel(small_ref, *smalls)


def hidden_back_kernel(mine_ref, other_ref, hid_ref, inv_ref, gain_ref, cot_ref, out_ref, gn_ref):
    d_normed = mine_ref[...].astype(F32) + other_ref[...].astype(F32)
    hid = hid_ref[...].astype(F32)
    inv = inv_ref[...]
    scaled = hid * inv
    gn_ref[...] = jnp.sum(d_normed * scaled, axis=0, keepdims=True)
    q = d_normed * gain_ref[...]
    mean = jnp.sum(q * scaled, axis=1, keepdims=True) / hid.shape[1]
    out_ref[...] = cot_ref[...].astype(F32) + inv * (q - scaled * mean)


def masks_of(seg_col, seg_row):
    rows = seg_col.shape[0]
    t = lax.broadcasted_iota(jnp.int32, (rows, rows), 0)
    s = lax.broadcasted_iota(jnp.int32, (rows, rows), 1)
    return jnp.where((t >= s) & (seg_col == seg_row), 0.0, -1e30).astype(F32)


def block_kernel(heads, x_ref, b_ref, c_ref, cum_ref, cumr_ref, dtr_ref, marks_ref, segs_ref, y_ref,
                 cb_ref, bias_ref):
    cb_ref[...] = mul(c_ref[...], b_ref[...], NT)
    bias_ref[...] = masks_of(marks_ref[:, 8:9], segs_ref[0:1])
    for h in range(0, heads, 2):
        lanes = slice(h * P_SIZE, h * P_SIZE + PAIR)
        parts = []
        for head in (h, h + 1):
            steps = decay_steps(cum_ref[...], cumr_ref[...], dtr_ref[...], bias_ref[...], head)
            parts.append(mul((steps * cb_ref[...]).astype(BF16), x_ref[:, lanes]))
        y_ref[:, lanes] = two(*parts)


def gate_kernel(pairs, yb_ref, x_ref, c_ref, cum_ref, marks_ref, z_ref, do_ref, skip_ref,
                gain_ref, s1_ref, s2_ref, y_ref, sums_ref):
    cum = cum_ref[...]
    marks = marks_ref[...]
    square = jnp.zeros((cum.shape[0], PAIR), F32)
    cross = square
    for p in range(pairs):
        lanes = slice(p * PAIR, (p + 1) * PAIR)
        entry = marks[:, 6:7] * jnp.exp(pair_of(cum, 2 * p))
        y_ssd = yb_ref[:, lanes] + entry * mul(c_ref[...], s1_ref[:, lanes] + s2_ref[:, lanes])
        y_ref[:, lanes] = y_ssd
        y = y_ssd + skip_ref[:, lanes] * x_ref[:, lanes].astype(F32)
        z = z_ref[:, lanes].astype(F32)
        gated = y * z * jax.nn.sigmoid(z)
        square = square + gated * gated
        cross = cross + gated * (do_ref[:, lanes] * gain_ref[:, lanes])
    lane = lax.broadcasted_iota(jnp.int32, (1, 2), 1)
    sums_ref[...] = jnp.where(
        lane == 0,
        jnp.sum(square, axis=1, keepdims=True),
        jnp.sum(cross, axis=1, keepdims=True),
    )


def norm_kernel(pairs, inner_full, y_ref, x_ref, c_ref, cum_ref, marks_ref, z_ref, do_ref, skip_ref,
                gain_ref, sums_ref, *refs):
    on_ref, dy_ref, dz_ref, gg_ref, back_ref, back16_ref = refs[-6:]
    cum = cum_ref[...]
    marks = marks_ref[...]
    rms = lax.rsqrt(sums_ref[:, 0:1] / inner_full + EPS)
    coef = rms * rms * sums_ref[:, 1:2] / inner_full
    for p in range(pairs):
        lanes = slice(p * PAIR, (p + 1) * PAIR)
        y = y_ref[:, lanes] + skip_ref[:, lanes] * x_ref[:, lanes].astype(F32)
        z = z_ref[:, lanes].astype(F32)
        sig = jax.nn.sigmoid(z)
        silu = z * sig
        normal = y * silu * rms
        d_out = do_ref[:, lanes]
        on_ref[:, lanes] = (normal * gain_ref[:, lanes]).astype(BF16)
        gg_ref[:, lanes] = jnp.sum(d_out * normal, axis=0, keepdims=True)
        d_gated = d_out * gain_ref[:, lanes] * rms - normal * coef
        d_y = (d_gated * silu).astype(BF16)
        dy_ref[:, lanes] = d_y
        dz_ref[:, lanes] = (d_gated * y * sig * (1.0 + z * (1.0 - sig))).astype(BF16)
        entry = marks[:, 6:7] * jnp.exp(pair_of(cum, 2 * p))
        back = mul(c_ref[...], (entry * d_y.astype(F32)).astype(BF16), TN)
        back_ref[:, lanes] = back
        back16_ref[:, lanes] = back.astype(BF16)


def block_back_kernel(heads, dy_ref, x_ref, b_ref, c_ref, cum_ref, cumr_ref, dtr_ref, marks_ref,
                      segs_ref, back_ref, db_ref, dc_ref, cb_ref, bias_ref, dcb_ref):
    cb_ref[...] = mul(c_ref[...], b_ref[...], NT)
    bias_ref[...] = masks_of(marks_ref[:, 8:9], segs_ref[0:1])
    lane = lax.broadcasted_iota(jnp.int32, (1, PAIR), 1)
    for h in range(0, heads, 2):
        lanes = slice(h * P_SIZE, h * P_SIZE + PAIR)
        d_y = dy_ref[:, lanes]
        x = x_ref[:, lanes]
        parts = []
        for head in (h, h + 1):
            steps = decay_steps(cum_ref[...], cumr_ref[...], dtr_ref[...], bias_ref[...], head)
            mix = (steps * cb_ref[...]).astype(BF16)
            own = (lane < P_SIZE) == (head == h)
            both = mul(jnp.where(own, d_y, jnp.zeros_like(d_y)), x, NT) * steps
            if head == 0:
                dcb_ref[...] = both
            else:
                dcb_ref[...] += both
            parts.append(mul(mix, d_y, TN))
        back_ref[:, lanes] = two(*parts)
    d_cb = dcb_ref[...].astype(BF16)
    dc_ref[...] = mul(d_cb, b_ref[...])
    db_ref[...] = mul(d_cb, c_ref[...], TN)


def state_back_kernel(heads, dy_ref, x_ref, b_ref, c_ref, cum_ref, dt_ref, marks_ref,
                      ub_ref, y_ref, db0_ref, dc0_ref, ext_ref, bcext_ref, tx_ref, bx_ref, tbc_ref,
                      bbc_ref, skip_ref, raw_ref, dtb_ref, alog_ref, pick_ref, g1_ref, g2_ref,
                      s1_ref, s2_ref, *refs):
    (shared_ref, rim_ref, rimbc_ref, dpre_ref, small_ref, skipg_ref, in_ref, out_ref, x_sum_ref,
     thr_ref) = refs[-10:]
    cum = cum_ref[...]
    dt = dt_ref[...]
    marks = marks_ref[...]
    rows = cum.shape[0]
    d_b = db0_ref[...]
    d_c = dc0_ref[...]
    for h in range(0, heads, 2):
        lanes = slice(h * P_SIZE, h * P_SIZE + PAIR)
        entry, tail = gains(cum, dt, marks, h)
        d_y16 = dy_ref[:, lanes]
        d_y = d_y16.astype(F32)
        x = x_ref[:, lanes].astype(F32)
        g = g1_ref[:, lanes] + g2_ref[:, lanes]
        s = s1_ref[:, lanes] + s2_ref[:, lanes]
        from_state = tail * mul(b_ref[...], g)
        ub = ub_ref[:, lanes]
        d_xs = skip_ref[:, lanes] * d_y + ub + from_state
        d_b = d_b + mul((tail * x).astype(BF16), g, NT)
        d_c = d_c + mul((entry * d_y).astype(BF16), s, NT)
        head_of = lax.broadcasted_iota(jnp.int32, (PAIR, heads), 0) // P_SIZE + h
        pick = (head_of == lax.broadcasted_iota(jnp.int32, (PAIR, heads), 1)).astype(BF16)

        def per_head(v):
            high = v.astype(BF16)
            low = (v - high.astype(F32)).astype(BF16)
            return mul(high, pick) + mul(low, pick)

        inside = per_head(d_y * y_ref[:, lanes] - x * ub)
        outside = per_head(x * from_state)
        along_x = per_head(x * ub)
        if h == 0:
            in_ref[...] = inside
            out_ref[...] = outside
            x_sum_ref[...] = along_x
        else:
            in_ref[...] += inside
            out_ref[...] += outside
            x_sum_ref[...] += along_x
        skipg_ref[:, lanes] = jnp.sum(d_y * x, axis=0, keepdims=True)
        both = per_head(jnp.sum(g.astype(F32) * s.astype(F32), axis=0, keepdims=True))
        if h == 0:
            thr_ref[...] = both
        else:
            thr_ref[...] += both
        pre = conv_pre(ext_ref[:, lanes].astype(F32), tx_ref[:, lanes], bx_ref[:, lanes], marks)
        sig = jax.nn.sigmoid(pre)
        d_pre = d_xs * sig * (1.0 + pre * (1.0 - sig))
        dpre_ref[:, lanes] = d_pre
        rim_ref[:, lanes] = d_pre[:8]
    last = cum[rows - 1 : rows]
    run_gain = marks[rows - 1 : rows, 6:7] * jnp.exp(last)
    through = run_gain * thr_ref[...]
    d_decay = (
        mul(tri(rows, upper=True), in_ref[...], precision=EXACT)
        + mul(tri(rows, strict=True), out_ref[...], precision=EXACT)
        + through
    )
    dt_in = raw_ref[...] + dtb_ref[...]
    sig = jax.nn.sigmoid(dt_in)
    ratio = jnp.where(dt_in < -20.0, 1.0, sig / jnp.maximum(dt, 1e-30))
    d_raw = (x_sum_ref[...] + out_ref[...]) * ratio - jnp.exp(alog_ref[...]) * d_decay * sig
    high = d_raw.astype(BF16)
    low = (d_raw - high.astype(F32)).astype(BF16)
    shared_ref[:, 2 * N :] = jnp.zeros((rows, TAIL - 2 * N), BF16)
    shared_ref[:, 2 * N : NBC] = (mul(high, pick_ref[...]) + mul(low, pick_ref[...])).astype(BF16)
    small_ref[...] = jnp.zeros(small_ref.shape, F32)
    small_ref[0:1, :heads] = jnp.sum(d_raw, axis=0, keepdims=True)
    small_ref[1:2, :heads] = -jnp.exp(alog_ref[...]) * jnp.sum(dt * d_decay, axis=0, keepdims=True)
    shared_ref[:, :N] = d_b.astype(BF16)
    shared_ref[:, N : 2 * N] = d_c.astype(BF16)
    pre = conv_pre(bcext_ref[...].astype(F32), tbc_ref[...], bbc_ref[...], marks)
    sig = jax.nn.sigmoid(pre)
    slope = sig * (1.0 + pre * (1.0 - sig))
    inner = heads * P_SIZE
    rimbc_ref[:, :N] = d_b[:8].astype(BF16).astype(F32) * slope[:8, :N]
    rimbc_ref[:, N:] = d_c[:8].astype(BF16).astype(F32) * slope[:8, N:]
    rim_ref[:, inner:] = rimbc_ref[...]


def taps_back(d_pre, rim, ext, taps, marks, dv_ref, lanes, grads_ref):
    rows = d_pre.shape[0]
    longer = jnp.concatenate([d_pre, rim], axis=0)
    d_v = taps[KC - 1 : KC] * d_pre
    for shift in range(1, KC):
        moved = pltpu.roll(longer, rows + 8 - shift, 0)[:rows]
        d_v = d_v + taps[KC - 1 - shift : KC - shift] * moved * marks[:, 2 + shift : 3 + shift]
    dv_ref[:, lanes] = d_v.astype(BF16)
    for k in range(KC):
        v = ext[RIM:] if k == KC - 1 else (
            pltpu.roll(ext, KC - 1 - k, 0)[RIM:] * marks[:, k : k + 1]
        )
        grads_ref[k : k + 1, lanes] = jnp.sum(d_pre * v, axis=0, keepdims=True)
    grads_ref[KC : KC + 1, lanes] = jnp.sum(d_pre, axis=0, keepdims=True)


def conv_back_kernel(pairs, dpre_ref, rim_ref, ext_ref, tx_ref, marks_ref, mine_ref, other_ref,
                     rimbc_ref, bcext_ref, tbc_ref, bbc_ref, dx_ref, grads_ref):
    inner = pairs * PAIR
    marks = marks_ref[...]
    for p in range(pairs):
        lanes = slice(p * PAIR, (p + 1) * PAIR)
        taps_back(dpre_ref[:, lanes], rim_ref[:, lanes], ext_ref[:, lanes].astype(F32),
                  tx_ref[:, lanes], marks, dx_ref, lanes, grads_ref)
    ext = bcext_ref[...].astype(F32)
    pre = conv_pre(ext, tbc_ref[...], bbc_ref[...], marks)
    sig = jax.nn.sigmoid(pre)
    shared = mine_ref[...].astype(F32) + other_ref[...].astype(F32)
    d_pre = shared[:, : 2 * N] * sig * (1.0 + pre * (1.0 - sig))
    taps_back(d_pre, rim_ref[:, inner:] + rimbc_ref[...], ext, tbc_ref[...], marks, dx_ref,
              slice(inner, inner + 2 * N), grads_ref)
    dx_ref[:, inner + 2 * N :] = shared[:, 2 * N :].astype(BF16)


def smalls_kernel(seqs, norm_ref, conv_ref, *refs):
    out_ref = refs[-1]
    head, skip, gate = (refs[i * seqs : (i + 1) * seqs] for i in range(3))
    inner = skip[0].shape[1]

    def total(parts):
        return functools.reduce(lambda a, b: a + b, [p[...] for p in parts])

    out_ref[KC + 1 :] = jnp.zeros((8 - KC - 1, out_ref.shape[1]), F32)
    out_ref[: KC + 1] = jnp.sum(conv_ref[:, : KC + 1], axis=0)
    out_ref[5:6, :inner] = jnp.sum(norm_ref[...], axis=0)
    out_ref[6:7, :inner] = total(gate)
    out_ref[7:8, :inner] = total(skip)
    both = total(head)
    out_ref[5:6, inner : inner + PAIR] = both[0:1]
    out_ref[6:7, inner : inner + PAIR] = both[1:2]


def smalls_out_kernel(all_ref, gn_ref, tx_ref, bx_ref, tbc_ref, bbc_ref, dtb_ref, alog_ref, skip_ref,
                      gg_ref):
    inner = gn_ref.shape[1]
    heads = dtb_ref.shape[1]
    tx_ref[...] = all_ref[:KC, :inner]
    tbc_ref[...] = all_ref[:KC, inner:]
    bx_ref[...] = all_ref[KC : KC + 1, :inner]
    bbc_ref[...] = all_ref[KC : KC + 1, inner:]
    gn_ref[...] = all_ref[5:6, :inner]
    gg_ref[...] = all_ref[6:7, :inner]
    dtb_ref[...] = all_ref[5:6, inner : inner + heads]
    alog_ref[...] = all_ref[6:7, inner : inner + heads]
    lane = lax.broadcasted_iota(jnp.int32, (inner, heads), 0) // P_SIZE
    pick = (lane == lax.broadcasted_iota(jnp.int32, (inner, heads), 1)).astype(F32)
    skip_ref[...] = mul(all_ref[7:8, :inner], pick, precision=EXACT)


def launch(order, kernel, name, ins, outs, scratch=(), grid=(1,), into=()):
    def spec(block, index):
        if block is None:
            return pl.BlockSpec(memory_space=pltpu.SMEM)
        return pl.BlockSpec(block, index)

    values = [a for a, _, _ in ins] + list(into)
    if order is not None:
        values = order.after(*values)
    results = pl.pallas_call(
        kernel,
        grid=grid,
        in_specs=[spec(block, index) for _, block, index in ins]
        + [pl.BlockSpec(memory_space=pl.ANY)] * len(into),
        out_specs=[spec(block, index) for _, block, index in outs],
        out_shape=[jax.ShapeDtypeStruct(*form) for form, _, _ in outs],
        scratch_shapes=list(scratch),
        input_output_aliases={len(ins) + i: i for i in range(len(into))},
        compiler_params=pltpu.CompilerParams(vmem_limit_bytes=VMEM),
        cost_estimate=pl.CostEstimate(flops=1, bytes_accessed=1, transcendentals=0),
        name=name,
    )(*values)
    if order is not None:
        order.did(results[0])
    return results


def at(a, b):
    return a, (None,) + a.shape[1:], lambda *_: (b,) + (0,) * (a.ndim - 1)


def own(a):
    return a, (None,) + a.shape[1:], lambda b: (b,) + (0,) * (a.ndim - 1)


def every(a):
    a = a.reshape((1, -1)) if a.ndim == 1 else a
    return a, a.shape, lambda *b: (0,) * a.ndim


def scalar(a):
    return a, None, None


def gives_at(shape, kind, b):
    return (shape, kind), (None,) + shape[1:], lambda *_: (b,) + (0,) * (len(shape) - 1)


def gives_whole(shape, kind):
    return (shape, kind), shape, lambda *b: (0,) * len(shape)


def head_parts(value):
    if lax.axis_size("head") == 2:
        return value, hop(value, "head", 1)
    return lax.psum(value, "head"), jnp.zeros_like(value)


def grads_begin(order, place, lefts, rights):
    wide = sum(r.shape[2] for r in rights)
    quarter = lefts[0].shape[2] // lax.axis_size("fsdp")
    half = quarter // 2
    return launch(
        order,
        functools.partial(weight_grad_kernel, len(lefts), lefts[0].shape[0]),
        "weight_grad",
        [scalar(place)] + [every(a) for a in lefts + rights],
        [
            gives_whole((quarter, wide), F32),
            gives_whole((half, wide), F32),
            gives_whole((half, wide), F32),
            gives_whole((quarter, wide), BF16),
            gives_whole((quarter, wide), BF16),
        ],
    )


def grads_first(terms):
    _, _, _, one, two_way = terms
    return hop(one, "fsdp", 1), hop(two_way, "fsdp", 2)


def grads_second(order, terms, first):
    _, low, high, _, _ = terms
    half = low.shape[0]
    low_one, high_two = order.after(*first)
    low_next = (low + low_one[half:].astype(F32)).astype(BF16)
    high_next = (high + high_two[half:].astype(F32)).astype(BF16)
    order.did(high_next)
    return hop(low_next, "fsdp", 2), hop(high_next, "fsdp", 1)


def grads_quarters(order, place, terms, first, second):
    mine = terms[0]
    quarter = (mine.shape[0] // 4, mine.shape[1])
    return launch(
        order,
        quarters_kernel,
        "quarters",
        [scalar(place)] + [every(a) for a in (mine, first[0], second[0], first[1], second[1])],
        [gives_whole(quarter, F32)] + [gives_whole(quarter, BF16)] * 3,
        [pltpu.VMEM(mine.shape, F32)],
    )


def grads_halves(order, place, terms, first, second):
    mine = terms[0]
    half = (mine.shape[0] // 2, mine.shape[1])
    return launch(
        order,
        halves_kernel,
        "halves",
        [scalar(place)] + [every(a) for a in (mine, first[0], second[0], first[1], second[1])],
        [gives_whole(half, F32), gives_whole(half, BF16)],
        [pltpu.VMEM(mine.shape, F32)],
    )


def line_quarter(order, place, keep, got):
    quarter = (keep.shape[0] // 2, keep.shape[1])
    own_sum, send = launch(
        order,
        quarter_kernel,
        "quarter",
        [scalar(place), every(keep), every(got)],
        [gives_whole(quarter, F32), gives_whole(quarter, BF16)],
    )
    return own_sum, hop(send, "seq", 2)


def line_join(order, place, mine, other):
    (both,) = launch(
        order,
        join_kernel,
        "join",
        [scalar(place), every(mine), every(other)],
        [gives_whole((2 * mine.shape[0], mine.shape[1]), BF16)],
    )
    return both


def small_sum(order, mine, other):
    (other,) = order.after(other)
    return order.did(mine + other)


def line_terms(quarters):
    return [hop(q, "seq", j) for j, q in enumerate(quarters[1:], 1)]


def line_sum(order, mine, terms):
    total = mine
    for term in order.after(*terms):
        total = total + term.astype(F32)
    return order.did(total.astype(BF16))


def line_parts(total):
    return [total] + [hop(total, "seq", j) for j in range(1, 4)]


def shards(
    hidden,
    segment_ids,
    norm_gain,
    w_zx,
    w_bcdt,
    conv_x,
    conv_x_bias,
    conv_bc,
    conv_bc_bias,
    dt_bias,
    a_log,
    d_skip,
    gate_gain,
    w_out,
    cotangent,
):
    head_place = lax.axis_index("head")
    head_count = lax.axis_size("head")
    seq_place = lax.axis_index("seq")
    seq_count = lax.axis_size("seq")
    place = jnp.stack([lax.axis_index("fsdp"), seq_place]).astype(jnp.int32)
    by_blocks = square("fsdp") and square("seq")
    seqs, rows, width = hidden.shape
    own_rows, _, inner = w_zx.shape
    heads = dt_bias.shape[0]
    inner_full = inner * head_count
    longer = rows + RIM
    pairs = heads // 2
    wide_x = inner + TAIL
    each = range(seqs)

    def gives(shape, kind):
        return ((seqs,) + shape, kind), (None,) + shape, lambda b: (b,) + (0,) * len(shape)

    order = Order()

    if by_blocks:
        half = own_rows // 2
        x_low, x_high = launch(
            order,
            pack_x_kernel,
            "pack_x",
            [every(w_zx), every(w_bcdt.T)],
            [gives_whole((half, wide_x), BF16)] * 2,
        )
        w_x = gather_halves(order, x_low, x_high, "fsdp")
    else:
        x_own = jnp.concatenate([w_zx[:, 1], jnp.pad(w_bcdt, ((0, 0), (0, TAIL - NBC)))], axis=1)
        w_x = lax.all_gather(x_own, "fsdp", axis=0, tiled=True)
        zo_own = jnp.concatenate([w_zx[:, 0], w_out.T], axis=1)
        w_zo = lax.all_gather(zo_own, "fsdp", axis=0, tiled=True)

    def input_norm(part):
        part = part.astype(F32)
        inv = lax.rsqrt(jnp.mean(part * part, axis=-1, keepdims=True) + EPS)
        return (part * inv * norm_gain).astype(BF16), inv

    before = step_along(hidden[:, rows - RIM :], "seq", 1)
    normed, inv_rms = input_norm(hidden)

    edge = KC - 1
    seg_ids, before = order.after(segment_ids, before)
    seg_padded = jnp.pad(seg_ids, ((0, 0), (edge, 0)), constant_values=-1)
    seg_padded = jnp.pad(seg_padded, ((0, 0), (0, edge)), constant_values=-2)
    seg_wide = lax.dynamic_slice_in_dim(seg_padded, seq_place * rows, rows + 2 * edge, 1).astype(F32)
    seg = seg_wide[:, edge : edge + rows]
    near = [seg] + [seg_wide[:, k : k + rows] for k in range(edge)]
    near += [seg_wide[:, edge + k : edge + k + rows] for k in range(1, KC)]
    near += [jnp.broadcast_to(s, seg.shape) for s in (seg_wide[:, edge - 1 : edge], seg[:, -1:])]
    segs = jnp.pad(jnp.stack(near, axis=1), ((0, 0), (0, 16 - len(near)), (0, 0)))
    head_pick = (
        jnp.arange(heads)[:, None] + head_place * heads == jnp.arange(NH)[None, :]
    ).astype(BF16)
    normed_rim, _ = input_norm(before)
    order.did(segs)
    (normed_rim,) = order.after(normed_rim)
    order.did(normed_rim)

    if by_blocks:
        (zo_own,) = launch(
            order,
            pack_zo_kernel,
            "pack_zo",
            [every(w_zx), every(w_out)],
            [gives_whole((own_rows, 2 * inner), BF16)],
        )
        zo_gathered = gather_first(zo_own, "fsdp")

    def project(b, into):
        if by_blocks:
            return launch(
                order,
                input_kernel,
                "input",
                [scalar(place), at(normed_rim, b), at(normed, b)] + [every(w) for w in w_x],
                [
                    gives_at((seqs, longer, inner), BF16, b),
                    gives_at((seqs, longer, 2 * N), BF16, b),
                    gives_at((seqs, rows, NH), BF16, b),
                ],
                into=into,
            )
        proj = jnp.dot(
            jnp.concatenate([normed_rim, normed], axis=1), w_x, preferred_element_type=F32
        ).astype(BF16)
        return (
            proj[..., :inner],
            proj[..., inner : inner + 2 * N],
            proj[:, RIM:, inner + 2 * N : inner + NBC],
        )

    conv_params = [every(conv_x), every(conv_x_bias), every(conv_bc), every(conv_bc_bias)]

    def convolve(b, x_ext, bc_ext, dt_all, into):
        return launch(
            order,
            functools.partial(conv_kernel, pairs),
            "conv",
            [at(x_ext, b), at(bc_ext, b), at(dt_all, b), every(head_pick), at(segs, b)]
            + conv_params
            + [every(dt_bias), every(a_log), every(d_skip)],
            [
                gives_at((seqs,) + shape, kind, b)
                for shape, kind in (
                    ((rows, inner), BF16),
                    ((rows, N), BF16),
                    ((rows, N), BF16),
                    ((rows, heads), F32),
                    ((rows, heads), F32),
                    ((heads, rows), F32),
                    ((heads, rows), F32),
                    ((rows, heads), F32),
                    ((rows, 16), F32),
                )
            ]
            + [
                gives_whole((1, inner), F32),
                gives_whole((N, inner), F32),
                gives_whole((N, inner), BF16),
                gives_whole((1, inner), F32),
            ],
            into=into,
        )

    def onward(lap, entered, moving, own_state, gain, steps):
        (moving,) = order.after(moving)
        entered = moving if entered is None else entered + moving
        leaving = order.did((gain * entered.astype(F32) + own_state).astype(BF16))
        return entered, pass_along(leaving, "seq", lap, steps)

    def nothing(state):
        return jnp.zeros(state.shape, BF16)

    def depart(sent, steps):
        if seq_count == 1:
            return None, nothing(sent)
        return None, pass_along(sent, "seq", 0, steps)

    def arrive(chain):
        entered, moving = chain
        return [nothing(moving) if entered is None else entered, moving]

    ext = ()
    parts = []
    moving = []
    for b in each:
        ext = project(b, ext)
        parts.append(convolve(b, *ext, parts[-1][:9] if parts else ()))
        moving.append(depart(parts[b][11], 1))
    xs, bs, cs, cum, dt, cum_rows, dt_rows, raw, marks = parts[-1][:9]
    run_gain, fresh, _, skips = zip(*[p[9:] for p in parts])
    skip = skips[0]

    square_form = pltpu.VMEM((rows, rows), F32)

    laps = range(1, seq_count - 1)
    for lap in laps[:1]:
        moving = [onward(lap, *moving[b], fresh[b], run_gain[b], 1) for b in each]
    if by_blocks:
        w_zo = gather_second(order, zo_own, zo_gathered, "fsdp")
    (y_block,) = launch(
        order,
        functools.partial(block_kernel, heads),
        "block",
        [own(a) for a in (xs, bs, cs, cum, cum_rows, dt_rows, marks, segs)],
        [gives((rows, inner), F32)],
        [square_form] * 2,
        grid=(seqs,),
    )
    for lap in laps[1:]:
        moving = [onward(lap, *moving[b], fresh[b], run_gain[b], 1) for b in each]
    state_in = [arrive(m) for m in moving]

    if by_blocks:
        z, d_outn = launch(
            order,
            gate_in_kernel,
            "gate_in",
            [scalar(place), own(normed), own(cotangent)] + [every(w) for w in w_zo],
            [gives((rows, inner), BF16), gives((rows, inner), F32)],
            grid=(seqs,),
        )
    else:
        z = jnp.dot(normed, w_zo[:, :inner], preferred_element_type=F32).astype(BF16)
        d_outn = jnp.dot(cotangent, w_zo[:, inner:], preferred_element_type=F32)

    def gate(b):
        y_ssd, sums = launch(
            order,
            functools.partial(gate_kernel, pairs),
            "gate",
            [at(a, b) for a in (y_block, xs, cs, cum, marks, z, d_outn)]
            + [every(skip), every(gate_gain), every(state_in[b][0]), every(state_in[b][1])],
            [gives_whole((rows, inner), F32), gives_whole((rows, 2), F32)],
        )
        return y_ssd, sum_all(sums, ("head",))

    def norm(b, y_ssd, sums, into):
        return launch(
            order,
            functools.partial(norm_kernel, pairs, inner_full),
            "norm",
            [every(y_ssd)]
            + [at(a, b) for a in (xs, cs, cum, marks, z, d_outn)]
            + [every(skip), every(gate_gain), every(sums)],
            [gives_at((seqs, rows, inner), BF16, b)] * 3
            + [
                gives_whole((1, inner), F32),
                gives_whole((N, inner), F32),
                gives_whole((N, inner), BF16),
            ],
            into=into,
        )

    y_ssd = []
    normals = []
    moving = []
    for b in each:
        y_b, sums = gate(b)
        y_ssd.append(y_b)
        normals.append(norm(b, y_b, sums, normals[-1][:3] if normals else ()))
        moving.append(depart(normals[b][5], -1))
    out_norm, d_y, d_z = normals[-1][:3]
    grad_gate, back, _ = zip(*[n[3:] for n in normals])

    x_ext, bc_ext, _ = ext


    def back_lap(lap):
        return [onward(lap, *moving[b], back[b], run_gain[b], -1) for b in each]

    if by_blocks:
        zo_terms = grads_begin(order, place, [normed, cotangent], [d_z, out_norm])
        zo_first = grads_first(zo_terms)
    for lap in laps[:1]:
        moving = back_lap(lap)
    back_x, d_b, d_c = launch(
        order,
        functools.partial(block_back_kernel, heads),
        "block_back",
        [own(a) for a in (d_y, xs, bs, cs, cum, cum_rows, dt_rows, marks, segs)],
        [gives((rows, inner), F32), gives((rows, N), F32), gives((rows, N), F32)],
        [square_form] * 3,
        grid=(seqs,),
    )
    for lap in laps[1:]:
        moving = back_lap(lap)
    if by_blocks:
        mixed, by_z = launch(
            order,
            output_kernel,
            "output",
            [scalar(place), own(out_norm), own(d_z)] + [every(w) for w in w_zo],
            [gives((rows, width), kind) for kind in (BF16, F32)],
            grid=(seqs,),
        )
    else:
        last = (((2,), (1,)), ((), ()))
        mixed = mul(out_norm, w_zo[:, inner:], last).astype(BF16)
        by_z = mul(d_z, w_zo[:, :inner], last)
    mixed, mixed_other = head_parts(mixed)
    grad_state = [arrive(m) for m in moving]

    def state_back(b, into):
        return launch(
            order,
            functools.partial(state_back_kernel, heads),
            "state_back",
            [at(a, b) for a in (d_y, xs, bs, cs, cum, dt, marks)]
            + [at(back_x, b), every(y_ssd[b]), at(d_b, b), at(d_c, b), at(x_ext, b), at(bc_ext, b)]
            + conv_params
            + [every(skip), at(raw, b)]
            + [every(a) for a in (dt_bias, a_log, head_pick, *grad_state[b], *state_in[b])],
            [
                gives_at((seqs, rows, TAIL), BF16, b),
                gives_at((seqs, 8, inner + 2 * N), F32, b),
                gives_at((seqs, 8, 2 * N), F32, b),
                gives_at((seqs, rows, inner), F32, b),
                gives_whole((2, PAIR), F32),
                gives_whole((1, inner), F32),
            ],
            [pltpu.VMEM((rows, heads), F32)] * 3 + [pltpu.VMEM((1, heads), F32)],
            into=into,
        )

    def neighbours(shared, rim, rim_bc):
        rim_other = jnp.zeros_like(rim_bc)
        for turn in range(1, head_count):
            rim_other = rim_other + lax.ppermute(
                rim_bc,
                ("seq", "head"),
                [
                    (s * head_count + p, (s - 1) * head_count + (p + turn) % head_count)
                    for s in range(1, seq_count)
                    for p in range(head_count)
                ],
            )
        return head_parts(shared) + (step_along(rim, "seq", -1), rim_other)

    state_parts = []
    together = ()
    for b in each:
        state_parts.append(state_back(b, together))
        together = state_parts[b][:4]
        if by_blocks and b == 0:
            zo_second = grads_second(order, zo_terms, zo_first)
    near_parts = neighbours(*together[:3])
    (block_out,) = launch(
        order,
        block_out_kernel,
        "block_out",
        [every(hidden), every(mixed), every(mixed_other)],
        [gives_whole((seqs, rows, width), BF16)],
    )
    if by_blocks:
        zo_keep, zo_send = grads_halves(order, place, zo_terms, zo_first, zo_second)
        zo_half = hop(zo_send, "seq", 1)
    shared, shared_other, rim, rim_other = near_parts
    d_xb, grad_conv = launch(
        order,
        functools.partial(conv_back_kernel, pairs),
        "conv_back",
        [own(together[3]), own(rim), own(x_ext), every(conv_x), own(marks)]
        + [own(a) for a in (shared, shared_other, rim_other, bc_ext)]
        + [every(conv_bc), every(conv_bc_bias)],
        [gives((rows, wide_x), BF16), gives((8, inner + 2 * N), F32)],
        grid=(seqs,),
    )
    small = [s[4] for s in state_parts]
    grad_skip = [s[5] for s in state_parts]

    if by_blocks:
        x_terms = grads_begin(order, place, [normed], [d_xb])
        x_first = grads_first(x_terms)
        (by_head,) = launch(
            order,
            functools.partial(input_back_kernel, head_count),
            "input_back",
            [scalar(place), own(d_xb), own(by_z)] + [every(w) for w in w_x],
            [gives((rows, width), BF16)],
            grid=(seqs,),
        )
    else:
        dxb = d_xb
        by_head = (
            by_z
            + mul(dxb[..., :inner], w_x[:, :inner], last)
            + mul(dxb[..., inner:], w_x[:, inner:], last) / head_count
        ).astype(BF16)
    by_head, by_other = head_parts(by_head)
    if by_blocks:
        zo_own, zo_quarter = line_quarter(order, place, zo_keep, zo_half)
        x_second = grads_second(order, x_terms, x_first)
    grad_hidden, grad_norm = launch(
        order,
        hidden_back_kernel,
        "hidden_back",
        [own(by_head), own(by_other), own(hidden), own(inv_rms), every(norm_gain), own(cotangent)],
        [gives((rows, width), F32), gives((1, width), F32)],
        grid=(seqs,),
    )

    (flat,) = launch(
        order,
        functools.partial(smalls_kernel, seqs),
        "smalls",
        [every(grad_norm), every(grad_conv)]
        + [every(a) for part in (small, grad_skip, grad_gate) for a in part],
        [gives_whole((8, inner + 2 * N), F32)],
    )

    small_forms = [
        gives_whole(shape, F32)
        for shape in (
            (1, width),
            (KC, inner),
            (1, inner),
            (KC, 2 * N),
            (1, 2 * N),
            (1, heads),
            (1, heads),
            (1, heads),
            (1, inner),
        )
    ]

    if by_blocks:
        small_hop = hop(flat, "fsdp", 1)
        zo_own = line_sum(order, zo_own, [zo_quarter])
        zo_quarter = hop(zo_own, "seq", 2)
        x_quarters = grads_quarters(order, place, x_terms, x_first, x_second)
        x_line = line_terms(x_quarters)
        (x_line[0],) = order.after(x_line[0])
        order.did(x_line[0])
        zo_mine = line_join(order, place, zo_own, zo_quarter)
        zo_other = hop(zo_mine, "seq", 1)
        flat = small_sum(order, flat, small_hop)
        flat = small_sum(order, flat, hop(flat, "fsdp", 2))
        (x_total,) = launch(
            order,
            line_sum_kernel,
            "line_sum",
            [every(a) for a in (x_quarters[0], *x_line, flat)],
            [gives_whole((own_rows // 4 + 16, wide_x), BF16)],
        )
        x_parts = line_parts(x_total)
        grad_z, grad_o = launch(
            order,
            finish_zo_kernel,
            "finish_zo",
            [scalar(place), every(zo_mine), every(zo_other)],
            [gives_whole((own_rows, inner), F32), gives_whole((inner, own_rows), F32)],
            [pltpu.VMEM((own_rows, 2 * inner), F32)],
        )
        grad_zx, grad_bcdt, *summed = launch(
            order,
            finish_x_kernel,
            "finish_x",
            [scalar(place), every(grad_z)] + [every(a) for a in x_parts],
            [gives_whole((own_rows, 2, inner), F32), gives_whole((NBC, own_rows), F32)]
            + small_forms,
            [pltpu.VMEM((8, inner + 2 * N), F32), pltpu.VMEM((own_rows, wide_x), F32)],
        )
        grad_bcdt = grad_bcdt.T
    else:
        flat = sum_all(flat, ("seq", "fsdp"))
        summed = launch(order, smalls_out_kernel, "smalls_out", [every(flat)], small_forms)
        def owned(left, right):
            full = lax.dot_general(
                left, right, (((0, 1), (0, 1)), ((), ())), preferred_element_type=F32
            )
            return lax.psum(lax.psum_scatter(full, "fsdp", scatter_dimension=0, tiled=True), "seq")

        grad_x = owned(normed, d_xb)
        grad_zx = jnp.stack([owned(normed, d_z), grad_x[:, :inner]], axis=1)
        grad_bcdt = grad_x[:, inner : inner + NBC]
        grad_o = owned(cotangent, out_norm).T
    grad_norm, grad_tx, grad_bx, grad_tbc, grad_bbc, grad_dtb, grad_alog, grad_skip, grad_gate = summed
    return (
        block_out,
        grad_hidden,
        grad_norm.reshape(-1),
        grad_zx,
        grad_bcdt,
        grad_tx,
        grad_bx.reshape(-1),
        grad_tbc,
        grad_bbc.reshape(-1),
        grad_dtb.reshape(-1),
        grad_alog.reshape(-1),
        grad_skip.reshape(-1),
        grad_gate.reshape(-1),
        grad_o,
    )


def solution(mesh):
    placed = (
        P("fsdp", "seq", None),
        P("fsdp", None),
        P(),
        P("fsdp", None, "head"),
        P("fsdp", None),
        P(None, "head"),
        P("head"),
        P(),
        P(),
        P("head"),
        P("head"),
        P("head"),
        P("head"),
        P("head", "fsdp"),
        P("fsdp", "seq", None),
    )
    return jax.shard_map(
        shards,
        mesh=mesh,
        in_specs=placed,
        out_specs=(
            P("fsdp", "seq", None),
            P("fsdp", "seq", None),
            P(),
            P("fsdp", None, "head"),
            P("fsdp", None),
            P(None, "head"),
            P("head"),
            P(),
            P(),
            P("head"),
            P("head"),
            P("head"),
            P("head"),
            P("head", "fsdp"),
        ),
        check_vma=False,
    )
```
